128 devices in a mesh: uly: 4 (over y_hi, core), blk: 32 (over y_lo, x, z).
Axes of the slice: x: 4, y: 4 (y_hi: 2, y_lo: 2; y = y_hi * 2 + y_lo), z: 4, core: 2. Of those that a mesh axis runs over, the one named last changes fastest.
Arguments:
- tokens: bfloat16 [16384, 1024], P(('uly', 'blk')), may hold values from -6 to 6
- document_ids: int32 [16384], replicated, may hold values from 0 to 3, as said below
- span_order: int32 [256], replicated, may hold values from 0 to 255, as said below
- attention_gain: bfloat16 [1024], P(('uly', 'blk')), may hold values from 0.5 to 1.5
- head_gain: bfloat16 [128], P(('uly', 'blk')), may hold values from 0.5 to 1.5
- qkv_weight: bfloat16 [1024, 2048], P(('uly', 'blk')), may hold values from -0.1875 to 0.1875
- out_weight: bfloat16 [1024, 1024], P(('uly', 'blk')), may hold values from -1.5 to 1.5
- feed_gain: bfloat16 [1024], P(('uly', 'blk')), may hold values from 0.5 to 1.5
- gate_weight: bfloat16 [1024, 4608], P(('uly', 'blk')), may hold values from -0.1875 to 0.1875
- up_weight: bfloat16 [1024, 4608], P(('uly', 'blk')), may hold values from -0.1875 to 0.1875
- down_weight: bfloat16 [4608, 1024], P(('uly', 'blk')), may hold values from -0.09375 to 0.09375
- cotangent: bfloat16 [16384, 1024], P(('uly', 'blk')), may hold values from -6 to 6
Outputs:
- block_output: bfloat16 [16384, 1024], P(('uly', 'blk'))
- grad_tokens: float32 [16384, 1024], P(('uly', 'blk'))
- grad_attention_gain: float32 [1024], P(('uly', 'blk'))
- grad_head_gain: float32 [128], P(('uly', 'blk'))
- grad_qkv_weight: float32 [1024, 2048], P(('uly', 'blk'))
- grad_out_weight: float32 [1024, 1024], P(('uly', 'blk'))
- grad_feed_gain: float32 [1024], P(('uly', 'blk'))
- grad_gate_weight: float32 [1024, 4608], P(('uly', 'blk'))
- grad_up_weight: float32 [1024, 4608], P(('uly', 'blk'))
- grad_down_weight: float32 [4608, 1024], P(('uly', 'blk'))
The draws below stay inside these ranges and needn't reach their ends.
Inputs may be any that keep to these rules, and one draw needn't show every extreme that they name: `document_ids`: Non-decreasing along the stream; all 4 documents occur; the first or the last document (which one drawn) holds 8192 tokens or more. `span_order`: A permutation of the stream blocks of 64 positions; row blocks 2 i and 2 i + 1 (device i's rows) hold stream blocks c and 255 - c in some order, for some c below 128.
All inputs are finite; a program needn't handle non-finite values.
Results may differ from the reference program's by a relative error of at most 0.04.
Values may be sent and summed in bfloat16 or wider, within the bound.
No kernel may reach another device: no remote copies, remote signals or barrier semaphores. Data moves between devices by JAX's collectives and lax.ppermute only.
A program may use at most 192 MiB of HBM per device.

```python
import math
import jax
import jax.numpy as jnp
from jax import lax

D = 1024
HEADS = 16
KV_HEADS = 8
HEAD_DIM = 64
FF = 4608
T_DEV = 128
SEQS = 4
TOKENS = 16384
SPANS = 256


def draw_document_ids(key, part):
    key = jax.random.fold_in(key, 11)
    key_one, key_two, key_three, key_four = jax.random.split(key, 4)
    long_length = TOKENS // 2 + jax.random.randint(key_one, (), 0, TOKENS // 4)
    remainder = TOKENS - long_length
    first_cut = jax.random.randint(key_two, (), 1, remainder - 1)
    second_cut = jax.random.randint(key_three, (), first_cut + 1, remainder)
    long_first = jax.random.randint(key_four, (), 0, 2)
    border_one = jnp.where(long_first == 1, long_length, first_cut)
    border_two = jnp.where(long_first == 1, long_length + first_cut, second_cut)
    border_three = jnp.where(long_first == 1, long_length + second_cut, remainder)
    stream = jnp.arange(TOKENS, dtype=jnp.int32)
    return (stream >= border_one).astype(jnp.int32) + (stream >= border_two).astype(jnp.int32) + (stream >= border_three).astype(jnp.int32)


def draw_span_order(key, part):
    key = jax.random.fold_in(key, 23)
    key_one, key_two = jax.random.split(key, 2)
    device_count = SPANS // 2
    lower_blocks = jax.random.permutation(key_one, device_count).astype(jnp.int32)
    paired = jnp.stack([lower_blocks, SPANS - 1 - lower_blocks], axis=1)
    flipped = jax.random.randint(key_two, (device_count, 1), 0, 2)
    paired = jnp.where(flipped == 1, paired[:, ::-1], paired)
    return paired.reshape(SPANS).astype(jnp.int32)


def block_levels(key, shape, cuts, least, largest):
    loudness, own = 1.0, jax.random.fold_in(key, 6)
    for axis_at, shards_of in cuts:
        draws = jnp.exp(jax.random.uniform(jax.random.fold_in(own, axis_at), (shards_of,), jnp.float32, least / len(cuts), largest / len(cuts)))
        loudness = loudness * jnp.repeat(draws, shape[axis_at] // shards_of).reshape([-1 if axis == axis_at else 1 for axis in range(len(shape))])
    return loudness


def centred(own_key, shape, scale, reach, cuts=(), kind=jnp.bfloat16):
    level = block_levels(own_key, shape, cuts, -0.22, 0.18) if cuts else 1.0
    result = jax.random.normal(own_key, shape, jnp.float32) * scale * level
    return jnp.minimum(jnp.maximum(result, -reach), reach).astype(kind)


def setup_inputs(seed: int = 0) -> dict:
    seeds = jax.random.split(jax.random.key(seed), 13)
    return {
        "tokens": centred(seeds[0], (TOKENS, D), 1.0, 6.0, ((0, 128),)),
        "document_ids": draw_document_ids(jax.random.fold_in(seeds[12], 71), 0),
        "span_order": draw_span_order(jax.random.fold_in(seeds[12], 71), 0),
        "attention_gain": jnp.clip(1.0 + 0.1 * jax.random.normal(seeds[3], (D,), jnp.float32), 0.5, 1.5).astype(jnp.bfloat16),
        "head_gain": jnp.clip(1.0 + 0.1 * jax.random.normal(seeds[4], (2 * HEAD_DIM,), jnp.float32), 0.5, 1.5).astype(jnp.bfloat16),
        "qkv_weight": centred(seeds[5], (D, (HEADS + 2 * KV_HEADS) * HEAD_DIM), D ** -0.5, 0.1875, ((0, 128),)),
        "out_weight": centred(seeds[6], (HEADS * HEAD_DIM, D), 16 ** -0.5, 1.5, ((0, 128),)),
        "feed_gain": jnp.clip(1.0 + 0.1 * jax.random.normal(seeds[7], (D,), jnp.float32), 0.5, 1.5).astype(jnp.bfloat16),
        "gate_weight": centred(seeds[8], (D, FF), D ** -0.5, 0.1875, ((0, 128),)),
        "up_weight": centred(seeds[9], (D, FF), D ** -0.5, 0.1875, ((0, 128),)),
        "down_weight": centred(seeds[10], (FF, D), FF ** -0.5, 0.09375, ((0, 128),)),
        "cotangent": centred(seeds[11], (TOKENS, D), 1.0, 6.0, ((0, 128),)),
    }


EPS = 1e-05
THETA = 1000000.0
NEGATIVE = -1e+30
HIGH = lax.Precision.HIGHEST

@jax.custom_vjp
def low(v):
    return lax.optimization_barrier(v.astype(jnp.bfloat16)).astype(jnp.float32)

@jax.custom_vjp
def low_back(v):
    return v

def low_keep(v):
    return (low(v), None)

def low_pass(kept, grad):
    return (grad,)

def back_keep(v):
    return (v, None)

def back_low(kept, grad):
    return (low(grad),)
low.defvjp(low_keep, low_pass)
low_back.defvjp(back_keep, back_low)

def rms_scale(values, gain):
    return values * lax.rsqrt(lax.optimization_barrier(jnp.mean(values * values, axis=-1, keepdims=True)) + EPS) * gain

def rotate(values, cosine_table, sine_table):
    middle = values.shape[-1] // 2
    turned = jnp.concatenate([-values[..., middle:], values[..., :middle]], axis=-1)
    return values * cosine_table + turned * sine_table

def rotary_tables(position):
    inverse = jnp.power(THETA, -jnp.arange(0, HEAD_DIM, 2).astype(jnp.float32) / HEAD_DIM)
    angles = position.astype(jnp.float32)[:, None] * inverse[None, :]
    angles = jnp.concatenate([angles, angles], axis=1)[:, None, :]
    return (jnp.cos(angles), jnp.sin(angles))

def attention(queries, keys_turned, values, stream, document):
    count_rows = queries.shape[0]
    block_rows = math.gcd(count_rows, 256)
    repeat = HEADS // KV_HEADS
    block_count = count_rows // block_rows
    query_blocks = queries.reshape(block_count, block_rows, KV_HEADS, repeat, HEAD_DIM)
    stream_blocks = stream.reshape(block_count, block_rows)
    document_blocks = document.reshape(block_count, block_rows)
    key_heads = keys_turned.reshape(count_rows, KV_HEADS, HEAD_DIM)
    value_heads = values.reshape(count_rows, KV_HEADS, HEAD_DIM)
    score_scale = HEAD_DIM ** (-0.5)

    def one_block(inputs):
        query_block, query_stream, query_document = inputs
        scores = low_back(jnp.einsum('qkgd,nkd->kgqn', query_block, key_heads, precision=HIGH) * score_scale)
        visible = (query_document[:, None] == document[None, :]) & (stream[None, :] <= query_stream[:, None])
        row_max = lax.optimization_barrier(jnp.max(jnp.where(visible, scores, NEGATIVE), axis=-1, keepdims=True))
        row_sum = lax.optimization_barrier(jnp.sum(jnp.exp(jnp.where(visible, scores - row_max, NEGATIVE)), axis=-1, keepdims=True))
        log_total = row_max + jnp.log(row_sum)
        probability = low(jnp.exp(jnp.where(visible, scores - log_total, NEGATIVE)))
        return jnp.einsum('kgqn,nkd->qkgd', probability, value_heads, precision=HIGH)
    attended = lax.map(jax.checkpoint(one_block), (query_blocks, stream_blocks, document_blocks))
    return attended.reshape(count_rows, HEADS * HEAD_DIM)

def reference(tokens, document_ids, span_order, attention_gain, head_gain, qkv_weight, out_weight, feed_gain, gate_weight, up_weight, down_weight, cotangent):
    half_rows = T_DEV // 2
    row_ids = jnp.arange(TOKENS, dtype=jnp.int32)
    stream = span_order[row_ids // half_rows] * half_rows + row_ids % half_rows
    starts = lax.optimization_barrier(jnp.sum((document_ids[None, :] < jnp.arange(SEQS, dtype=jnp.int32)[:, None]).astype(jnp.int32), axis=1))
    document = document_ids[stream]
    position = stream - starts[document]
    cosine_table, sine_table = rotary_tables(position)
    query_end = HEADS * HEAD_DIM
    key_end = query_end + KV_HEADS * HEAD_DIM

    def forward(input_value, gain_attention, gain_heads, weight_qkv, weight_out, gain_feed, weight_gate, weight_up, weight_down):
        count_rows = input_value.shape[0]
        normed = low(rms_scale(input_value, gain_attention))
        projected = low_back(jnp.dot(normed, weight_qkv, precision=HIGH))
        queries = rotate(rms_scale(projected[:, :query_end].reshape(count_rows, HEADS, HEAD_DIM), gain_heads[:HEAD_DIM]), cosine_table, sine_table)
        keys_turned = rotate(rms_scale(projected[:, query_end:key_end].reshape(count_rows, KV_HEADS, HEAD_DIM), gain_heads[HEAD_DIM:]), cosine_table, sine_table)
        queries = low_back(low(queries.reshape(count_rows, query_end)))
        keys_turned = low_back(low(keys_turned.reshape(count_rows, KV_HEADS * HEAD_DIM)))
        values = low_back(low(projected[:, key_end:]))
        attended = low_back(low(attention(queries, keys_turned, values, stream, document)))
        residual = input_value + low_back(jnp.dot(attended, weight_out, precision=HIGH))
        feed_normed = low(rms_scale(residual, gain_feed))
        gate_value = low_back(jnp.dot(feed_normed, weight_gate, precision=HIGH))
        upward = low_back(jnp.dot(feed_normed, weight_up, precision=HIGH))
        hidden = low(jax.nn.silu(gate_value) * upward)
        return residual + low_back(jnp.dot(hidden, weight_down, precision=HIGH))
    output, pull_back = jax.vjp(forward, tokens.astype(jnp.float32), attention_gain.astype(jnp.float32), head_gain.astype(jnp.float32), qkv_weight.astype(jnp.float32), out_weight.astype(jnp.float32), feed_gain.astype(jnp.float32), gate_weight.astype(jnp.float32), up_weight.astype(jnp.float32), down_weight.astype(jnp.float32))
    gradients = pull_back(cotangent.astype(jnp.float32))
    return (output.astype(jnp.bfloat16), gradients[0], gradients[1], gradients[2], gradients[3], gradients[4], gradients[5], gradients[6], gradients[7], gradients[8])
```

```python
import functools

import jax
import jax.numpy as jnp
from jax import lax
from jax.experimental import pallas as pl
from jax.experimental.pallas import tpu as pltpu
from jax.sharding import Mesh
from jax.sharding import PartitionSpec as P

F32 = jnp.float32
BF16 = jnp.bfloat16
HEADS = 16
KV_HEADS = 8
HEAD_DIM = 64
SEQS = 4
SPAN = 64
EPS = 1e-05
THETA = 1000000.0
LOG2E = 1.4426950408889634
LN2 = 0.6931471805599453
SCORE_SCALE = HEAD_DIM ** -0.5

AXES = ("h", "c", "l", "x", "z")
RING = ("h", "c", "l")
PLANE = ("x", "z")
OFFSETS = (0, -1, 1, 2)

TILE, PAIR, UNROLL, PIECES = 1024, 2, 2, 8
PAIR_ROWS = 2 * SPAN


def dot_nn(left, right):
    return lax.dot_general(left, right, (((1,), (0,)), ((), ())), preferred_element_type=F32)


def dot_nt(left, right):
    return lax.dot_general(left, right, (((1,), (1,)), ((), ())), preferred_element_type=F32)


def dot_tn(left, right):
    return lax.dot_general(left, right, (((0,), (0,)), ((), ())), preferred_element_type=F32)


def transposed(values):
    return values.astype(F32).T


def heads_beside(block):
    turned = transposed(block)
    return jnp.concatenate([turned[:HEAD_DIM], turned[HEAD_DIM:]], axis=1)


def heads_back(turned):
    return jnp.concatenate([turned[:, :SPAN], turned[:, SPAN:]], axis=0).T


def fetch(pieces, raw_s, sem):
    rows = pieces[0].shape[0]
    return [
        pltpu.make_async_copy(piece, raw_s.at[pl.ds(k * rows, rows)], sem.at[k]) for k, piece in enumerate(pieces)
    ]


def sort_keys(slot_ref, raw_s, kv_s, kvt_s):
    per = 8

    def one(group, carry):
        found = []
        for k in range(per):
            source = pl.multiple_of(slot_ref[group * per + k] * SPAN, SPAN)
            found.append(raw_s[pl.ds(source, SPAN), :])
        block = jnp.concatenate(found, axis=0)
        first = pl.multiple_of(group * per * SPAN, per * SPAN)
        kv_s[pl.ds(first, per * SPAN), :] = block
        kvt_s[:, pl.ds(first, per * SPAN)] = transposed(block).astype(BF16)
        return carry

    lax.fori_loop(0, raw_s.shape[0] // (SPAN * per), one, 0)


def row_limits(blocks, stream_ref, starts_ref, limit_s):
    half = stream_ref.shape[0] // 2
    for i in range(blocks):
        block = stream_ref[i if i < blocks // 2 else half + i - blocks // 2]
        position = block * SPAN + (lax.broadcasted_iota(jnp.int32, (1, PAIR_ROWS), 1) & (SPAN - 1))
        begin = jnp.zeros((1, PAIR_ROWS), jnp.int32)
        for number in range(1, SEQS):
            begin = jnp.where(position >= starts_ref[number], starts_ref[number], begin)
        limit_s[i, 0:1] = begin
        limit_s[i, 1:2] = position
    limit_s[blocks, 0:1] = jnp.ones((1, PAIR_ROWS), jnp.int32)
    limit_s[blocks, 1:2] = jnp.zeros((1, PAIR_ROWS), jnp.int32)


def visible(item, first, limit_s):
    key = lax.broadcasted_iota(jnp.int32, (TILE, PAIR_ROWS), 0)
    return (key >= limit_s[item, 0:1] - first) & (key <= limit_s[item, 1:2] - first)


def forward_kernel(stream_ref, slot_ref, item_ref, tile_ref, count_ref, starts_ref, q_ref, *refs):
    pieces = refs[:PIECES]
    o_ref, low_ref, l_ref, raw_s, kv_s, kvt_s, qt_s, acc_s, sum_s, limit_s, sem = refs[PIECES:]
    blocks = q_ref.shape[0] // SPAN
    copies = fetch(pieces, raw_s, sem)
    for copy in copies:
        copy.start()
    for i in range(blocks):
        qt_s[i, :HEAD_DIM] = heads_beside(q_ref[pl.ds(i * SPAN, SPAN), :]).astype(BF16)
        qt_s[i, HEAD_DIM:] = jnp.zeros((HEAD_DIM, PAIR_ROWS), BF16)
    qt_s[blocks] = jnp.zeros((2 * HEAD_DIM, PAIR_ROWS), BF16)
    row_limits(blocks, stream_ref, starts_ref, limit_s)
    acc_s[...] = jnp.zeros(acc_s.shape, F32)
    sum_s[...] = jnp.zeros(sum_s.shape, F32)
    for copy in copies:
        copy.wait()
    sort_keys(slot_ref, raw_s, kv_s, kvt_s)

    def step(group, carry):
        found = []
        for u in range(UNROLL):
            at = group * UNROLL + u
            items = [item_ref[at * PAIR + k] for k in range(PAIR)]
            first = pl.multiple_of(tile_ref[at] * TILE, TILE)
            right = jnp.concatenate([qt_s[i] for i in items], axis=1)
            scores = dot_nn(kv_s[pl.ds(first, TILE), :], right)
            seen = jnp.concatenate([visible(i, first, limit_s) for i in items], axis=1)
            weights = jnp.where(seen, jnp.exp2(scores), 0.0)
            update = dot_nn(kvt_s[HEAD_DIM:, pl.ds(first, TILE)], weights.astype(BF16))
            part = jnp.sum(weights.reshape(TILE // 8, 8, PAIR * PAIR_ROWS), axis=0)
            found.append((items, update, part))
        for items, update, part in found:
            for k, i in enumerate(items):
                at = slice(k * PAIR_ROWS, (k + 1) * PAIR_ROWS)
                acc_s[i] += update[:, at]
                sum_s[i] += part[:, at]
        return carry

    lax.fori_loop(0, lax.div(count_ref[0] + (UNROLL - 1), UNROLL), step, 0)
    for i in range(blocks):
        total = jnp.sum(sum_s[i], axis=0, keepdims=True)
        result = heads_back(acc_s[i] * (1.0 / total))
        o_ref[pl.ds(i * SPAN, SPAN), :] = result
        low_ref[pl.ds(i * SPAN, SPAN), :] = result.astype(BF16)
        l_ref[i] = jnp.broadcast_to(jnp.log2(total), (8, PAIR_ROWS))


def backward_kernel(
    stream_ref, slot_ref, item_ref, tile_ref, count_ref, starts_ref, q_ref, do_ref, o_ref, l_ref, *refs
):
    pieces, dq_ref, outs = refs[:PIECES], refs[PIECES], refs[PIECES + 1 : 2 * PIECES + 1]
    raw_s, kv_s, kvt_s, left_s, right_s, stat_s, limit_s, dq_s, dkv_s, sem = refs[2 * PIECES + 1 :]
    blocks = q_ref.shape[0] // SPAN
    copies = fetch(pieces, raw_s, sem)
    for copy in copies:
        copy.start()
    nothing = jnp.zeros((HEAD_DIM, PAIR_ROWS), F32)
    for i in range(blocks):
        rows = pl.ds(i * SPAN, SPAN)
        grad_out = heads_beside(do_ref[rows, :])
        query_side = jnp.concatenate([heads_beside(q_ref[rows, :]), nothing], axis=0)
        grad_side = jnp.concatenate([nothing, grad_out], axis=0)
        right_s[i, :, :PAIR_ROWS] = query_side.astype(BF16)
        right_s[i, :, PAIR_ROWS:] = grad_side.astype(BF16)
        left_s[i, :PAIR_ROWS] = query_side.T.astype(BF16)
        left_s[i, PAIR_ROWS:] = grad_side.T.astype(BF16)
        stat_s[i, 0:1] = l_ref[i][0:1]
        stat_s[i, 1:2] = jnp.sum(grad_out * heads_beside(o_ref[rows, :]), axis=0, keepdims=True)
    left_s[blocks] = jnp.zeros(left_s.shape[1:], BF16)
    right_s[blocks] = jnp.zeros(right_s.shape[1:], BF16)
    stat_s[blocks] = jnp.zeros(stat_s.shape[1:], F32)
    row_limits(blocks, stream_ref, starts_ref, limit_s)
    dq_s[...] = jnp.zeros(dq_s.shape, F32)

    def clear(block, carry):
        dkv_s[pl.ds(pl.multiple_of(block * TILE, TILE), TILE), :] = jnp.zeros((TILE, 2 * HEAD_DIM), F32)
        return carry

    lax.fori_loop(0, kv_s.shape[0] // TILE, clear, 0)
    for copy in copies:
        copy.wait()
    sort_keys(slot_ref, raw_s, kv_s, kvt_s)

    def step(group, carry):
        found = []
        for u in range(UNROLL):
            at = group * UNROLL + u
            items = [item_ref[at * PAIR + k] for k in range(PAIR)]
            first = pl.multiple_of(tile_ref[at] * TILE, TILE)
            keys = kv_s[pl.ds(first, TILE), :]
            mixed, grads = [], []
            for i in items:
                both = dot_nn(keys, right_s[i])
                weights = jnp.exp2(both[:, :PAIR_ROWS] - stat_s[i, 0:1])
                weights = jnp.where(visible(i, first, limit_s), weights, 0.0)
                grad = (weights * (both[:, PAIR_ROWS:] - stat_s[i, 1:2])).astype(BF16)
                grads.append(grad)
                mixed += [grad, weights.astype(BF16)]
            update = dot_nn(kvt_s[:HEAD_DIM, pl.ds(first, TILE)], jnp.concatenate(grads, axis=1))
            left = jnp.concatenate([left_s[i] for i in items], axis=0)
            found.append((items, first, update, dot_nn(jnp.concatenate(mixed, axis=1), left)))
        for items, first, update, fresh in found:
            for k, i in enumerate(items):
                dq_s[i] += update[:, k * PAIR_ROWS : (k + 1) * PAIR_ROWS]
            dkv_s[pl.ds(first, TILE), :] += fresh
        return carry

    lax.fori_loop(0, lax.div(count_ref[0] + (UNROLL - 1), UNROLL), step, 0)
    for i in range(blocks):
        dq_ref[pl.ds(i * SPAN, SPAN), :] = heads_back(dq_s[i]) * SCORE_SCALE
    lane = lax.broadcasted_iota(jnp.int32, (1, 2 * HEAD_DIM), 1)
    scale = jnp.where(lane < HEAD_DIM, LN2, 1.0)
    rows = outs[0].shape[0]
    for k, out in enumerate(outs):

        def one(group, carry, k=k, out=out):
            for u in range(8):
                block = group * 8 + u
                source = pl.multiple_of(stream_ref[k * (rows // SPAN) + block] * SPAN, SPAN)
                target = pl.multiple_of(block * SPAN, SPAN)
                out[pl.ds(target, SPAN), :] = (dkv_s[pl.ds(source, SPAN), :] * scale).astype(BF16)
            return carry

        lax.fori_loop(0, rows // SPAN // 8, one, 0)


IN_VMEM = pl.BlockSpec(memory_space=pltpu.VMEM)
ANYWHERE = pl.BlockSpec(memory_space=pl.ANY)


def attention_forward(tables, queries, pieces):
    rows, part = queries.shape[0], pieces[0].shape[0]
    blocks, total = rows // SPAN, PIECES * part
    return pl.pallas_call(
        forward_kernel,
        grid_spec=pltpu.PrefetchScalarGridSpec(
            num_scalar_prefetch=6,
            grid=(),
            in_specs=[IN_VMEM] + [ANYWHERE] * PIECES,
            out_specs=[IN_VMEM] * 3,
            scratch_shapes=[
                pltpu.VMEM((total, 128), BF16),
                pltpu.VMEM((total, 128), BF16),
                pltpu.VMEM((128, total), BF16),
                pltpu.VMEM((blocks + 1, 128, 128), BF16),
                pltpu.VMEM((blocks + 1, HEAD_DIM, 128), F32),
                pltpu.VMEM((blocks + 1, 8, 128), F32),
                pltpu.VMEM((blocks + 1, 8, 128), jnp.int32),
                pltpu.SemaphoreType.DMA((PIECES,)),
            ],
        ),
        out_shape=[
            jax.ShapeDtypeStruct((rows, 128), F32),
            jax.ShapeDtypeStruct((rows, 128), BF16),
            jax.ShapeDtypeStruct((blocks, 8, 128), F32),
        ],
        compiler_params=pltpu.CompilerParams(vmem_limit_bytes=48 * 2**20),
        cost_estimate=pl.CostEstimate(flops=20 * 10**9, bytes_accessed=6 * 10**6, transcendentals=10**7),
        name="attention_forward",
    )(*tables, queries, *pieces)


def attention_backward(tables, queries, grad_out, outputs, logs, pieces):
    rows, part = queries.shape[0], pieces[0].shape[0]
    blocks, total = rows // SPAN, PIECES * part
    return pl.pallas_call(
        backward_kernel,
        grid_spec=pltpu.PrefetchScalarGridSpec(
            num_scalar_prefetch=6,
            grid=(),
            in_specs=[IN_VMEM] * 4 + [ANYWHERE] * PIECES,
            out_specs=[IN_VMEM] * (1 + PIECES),
            scratch_shapes=[
                pltpu.VMEM((total, 128), BF16),
                pltpu.VMEM((total, 128), BF16),
                pltpu.VMEM((128, total), BF16),
                pltpu.VMEM((blocks + 1, 256, 128), BF16),
                pltpu.VMEM((blocks + 1, 128, 256), BF16),
                pltpu.VMEM((blocks + 1, 8, 128), F32),
                pltpu.VMEM((blocks + 1, 8, 128), jnp.int32),
                pltpu.VMEM((blocks + 1, HEAD_DIM, 128), F32),
                pltpu.VMEM((total, 128), F32),
                pltpu.SemaphoreType.DMA((PIECES,)),
            ],
        ),
        out_shape=[jax.ShapeDtypeStruct((rows, 128), F32)] + [jax.ShapeDtypeStruct((part, 128), BF16)] * PIECES,
        compiler_params=pltpu.CompilerParams(vmem_limit_bytes=56 * 2**20),
        cost_estimate=pl.CostEstimate(flops=40 * 10**9, bytes_accessed=10**7, transcendentals=10**7),
        name="attention_backward",
    )(*tables, queries, grad_out, outputs, logs, *pieces)


def work_list(blocks, starts, total):
    count, tiles = blocks.shape[0], total // TILE
    first = blocks * SPAN
    begin = jnp.zeros_like(first)
    for number in range(1, SEQS):
        begin = jnp.where(first >= starts[number], starts[number], begin)
    shift = TILE.bit_length() - 1
    number = jnp.arange(tiles, dtype=jnp.int32)
    active = (number[:, None] >= (begin >> shift)[None, :]) & (number[:, None] <= (first >> shift)[None, :])
    flags = active.astype(jnp.int32)
    index = jnp.arange(count, dtype=jnp.int32)
    before = (index[:, None] < index[None, :]).astype(jnp.int32)
    rank = jnp.where(active, jnp.sum(flags[:, :, None] * before[None], axis=1), -1)
    groups = (jnp.sum(flags, axis=1) + (PAIR - 1)) >> (PAIR.bit_length() - 1)
    upto = (number[:, None] <= number[None, :]).astype(jnp.int32)
    ends = jnp.sum(groups[:, None] * upto, axis=0)
    most = -(-(tiles * (count // PAIR)) // UNROLL) * UNROLL
    group = jnp.arange(most, dtype=jnp.int32)
    past = group[:, None] >= ends[None, :]
    tile = jnp.sum(past.astype(jnp.int32), axis=1)
    base = jnp.sum(jnp.where(past, groups[None, :], 0), axis=1)
    mine = tile[:, None] == number[None, :]
    ranks = jnp.sum(jnp.where(mine[:, :, None], rank[None] + 1, 0), axis=1) - 1
    want = (group - base)[:, None] * PAIR + jnp.arange(PAIR, dtype=jnp.int32)[None, :]
    hit = ranks[:, None, :] == want[:, :, None]
    item = count - jnp.sum(jnp.where(hit, (count - index)[None, None, :], 0), axis=2)
    return item.reshape(-1), jnp.where(tile < tiles, tile, 0), ends[-1:]


def rotated(values):
    lane = lax.broadcasted_iota(jnp.int32, values.shape, 1)
    up = pltpu.roll(values, 32, 1)
    down = pltpu.roll(values, 96, 1)
    return jnp.where((lane & 63) < 32, -down, up)


def head_mean(values):
    size = values.shape[1]
    row = lax.broadcasted_iota(jnp.int32, (size, size), 0)
    column = lax.broadcasted_iota(jnp.int32, (size, size), 1)
    same = jnp.where((row >> 6) == (column >> 6), 1.0 / HEAD_DIM, 0.0).astype(BF16)
    high = values.astype(BF16)
    low = (values - high.astype(F32)).astype(BF16)
    return dot_nn(high, same) + dot_nn(low, same)


def project_kernel(ids_ref, x_ref, w_ref, cos_ref, sin_ref, gain_ref, n_ref, p_ref, q_ref, kv_ref):
    rows = cos_ref.shape[0] // ids_ref.shape[0]
    step = pl.program_id(0)
    places = []
    for k in range(x_ref.shape[0] // rows):
        member = ids_ref[step * (x_ref.shape[0] // rows) + k]
        places.append(pl.ds(pl.multiple_of(member * rows, rows), rows))
    values = x_ref[...].astype(F32)
    normed = (values * lax.rsqrt(jnp.mean(values * values, axis=1, keepdims=True) + EPS)).astype(BF16)
    projected = dot_nn(normed, w_ref[...])
    heads = projected * lax.rsqrt(head_mean(projected * projected) + EPS) * gain_ref[...]
    cosine = jnp.concatenate([cos_ref[at, :] for at in places], axis=0)
    sine = jnp.concatenate([sin_ref[at, :] for at in places], axis=0)
    query, key = heads[:, :128], heads[:, 128:]
    query = (query * cosine + rotated(query) * sine) * (SCORE_SCALE * LOG2E)
    key = key * cosine + rotated(key) * sine
    lane = lax.broadcasted_iota(jnp.int32, key.shape, 1)
    key = jnp.where(lane < HEAD_DIM, key, projected[:, 128:])
    for k, at in enumerate(places):
        mine = slice(k * rows, (k + 1) * rows)
        n_ref[at, :] = normed[mine]
        p_ref[at, :] = projected[mine]
        q_ref[at, :] = query[mine].astype(BF16)
        kv_ref[at, :] = key[mine].astype(BF16)


def project_back_kernel(ids_ref, dq_ref, dkv_ref, p_ref, cos_ref, sin_ref, gain_ref, w_ref, gp_ref, parts_ref, gg_ref):
    rows = cos_ref.shape[0] // ids_ref.shape[0]
    count = parts_ref.shape[0] // rows
    places = []
    for k in range(count):
        member = ids_ref[pl.program_id(0) * count + k]
        places.append(pl.ds(pl.multiple_of(member * rows, rows), rows))

    def read(ref):
        return jnp.concatenate([ref[at, :] for at in places], axis=0)

    cosine, sine, values = read(cos_ref), read(sin_ref), read(p_ref)
    query = read(dq_ref).astype(BF16).astype(F32)
    key = read(dkv_ref).astype(BF16).astype(F32)
    upstream = jnp.concatenate(
        [query * cosine - rotated(query) * sine, key * cosine - rotated(key) * sine], axis=1
    )
    scale = lax.rsqrt(head_mean(values * values) + EPS)
    weighted = upstream * gain_ref[...]
    inner = head_mean(values * weighted)
    back = scale * weighted - values * (scale * scale * scale) * inner
    lane = lax.broadcasted_iota(jnp.int32, key.shape, 1)
    back = jnp.concatenate([back[:, :128], jnp.where(lane < HEAD_DIM, back[:, 128:], key)], axis=1)
    back = back.astype(BF16)
    for k, at in enumerate(places):
        gp_ref[at, :] = back[k * rows : (k + 1) * rows]
    parts_ref[...] = dot_nt(back, w_ref[...]).astype(BF16)

    @pl.when(pl.program_id(0) == 0)
    def _():
        gg_ref[...] = jnp.zeros(gg_ref.shape, F32)

    terms = upstream * values * scale
    gg_ref[...] += jnp.sum(terms.reshape(-1, 8, terms.shape[1]), axis=0)


def by_slot(rows, width):
    return pl.BlockSpec((rows, width), lambda i, ids: (i, 0))


def whole_block(shape):
    return pl.BlockSpec(shape, lambda i, ids: (0, 0))


def project(ids, tokens, weight, cosine, sine, gains):
    total, width = tokens.shape
    steps = ids.shape[0] // 2
    return pl.pallas_call(
        project_kernel,
        grid_spec=pltpu.PrefetchScalarGridSpec(
            num_scalar_prefetch=1,
            grid=(steps,),
            in_specs=[
                by_slot(total // steps, width), whole_block(weight.shape), whole_block((total, 128)),
                whole_block((total, 128)), whole_block((1, 256)),
            ],
            out_specs=[whole_block((total, wide)) for wide in (width, 256, 128, 128)],
        ),
        out_shape=[
            jax.ShapeDtypeStruct((total, width), BF16),
            jax.ShapeDtypeStruct((total, 256), F32),
            jax.ShapeDtypeStruct((total, 128), BF16),
            jax.ShapeDtypeStruct((total, 128), BF16),
        ],
        compiler_params=pltpu.CompilerParams(vmem_limit_bytes=24 * 2**20),
        cost_estimate=pl.CostEstimate(flops=10**9, bytes_accessed=8 * 10**6, transcendentals=10**5),
        name="project",
    )(ids, tokens, weight, cosine, sine, gains)


def project_back(ids, grad_q, grad_kv, projected, cosine, sine, gains, weight):
    total, width = grad_q.shape[0], weight.shape[0]
    steps = ids.shape[0] // 2
    return pl.pallas_call(
        project_back_kernel,
        grid_spec=pltpu.PrefetchScalarGridSpec(
            num_scalar_prefetch=1,
            grid=(steps,),
            in_specs=[whole_block((total, wide)) for wide in (128, 128, 256, 128, 128)]
            + [whole_block((1, 256)), whole_block(weight.shape)],
            out_specs=[whole_block((total, 256)), by_slot(total // steps, width), whole_block((8, 256))],
        ),
        out_shape=[
            jax.ShapeDtypeStruct((total, 256), BF16),
            jax.ShapeDtypeStruct((total, width), BF16),
            jax.ShapeDtypeStruct((8, 256), F32),
        ],
        compiler_params=pltpu.CompilerParams(vmem_limit_bytes=24 * 2**20),
        cost_estimate=pl.CostEstimate(flops=10**9, bytes_accessed=8 * 10**6, transcendentals=10**5),
        name="project_back",
    )(ids, grad_q, grad_kv, projected, cosine, sine, gains, weight)


def out_back_kernel(ids_ref, a_ref, *refs):
    *near, far_ref, out_ref = refs
    rows = near[0].shape[0]
    total = jnp.zeros(out_ref.shape, F32)
    for k in range(2 * len(near)):
        block = near[k][...] if k < len(near) else far_ref[pl.ds((k - len(near)) * rows, rows), :]
        mine = a_ref[pl.ds(pl.multiple_of(ids_ref[k] * rows, rows), rows), :]
        total += dot_nn(transposed(mine).astype(BF16), block)
    out_ref[...] = total.astype(BF16)


def out_back(ids, attended, near, far):
    return pl.pallas_call(
        out_back_kernel,
        in_specs=[pl.BlockSpec(memory_space=pltpu.SMEM)] + [IN_VMEM] * (2 + len(near)),
        out_specs=IN_VMEM,
        out_shape=jax.ShapeDtypeStruct((attended.shape[1], far.shape[1]), BF16),
        compiler_params=pltpu.CompilerParams(vmem_limit_bytes=16 * 2**20),
        cost_estimate=pl.CostEstimate(flops=3 * 10**8, bytes_accessed=3 * 10**6, transcendentals=0),
        name="out_back",
    )(ids, attended, *near, far)


def feed_kernel(ids_ref, x_ref, c_ref, w_ref, h_ref, gg_ref, gu_ref, parts_ref, down_ref, wg_s, wu_s, wd_s):
    plane, packed, ff = w_ref.shape
    width = wg_s.shape[0]
    ring = width // (8 * plane)
    rows = wd_s.shape[0] // plane
    half = width // 2
    padded = (packed - 16 * ring) // 2

    @pl.when(pl.program_id(0) == 0)
    def _():
        for a in range(ring):
            for b in range(0, plane, 2):
                one = w_ref[b, pl.ds(a * 16, 16), :].astype(F32)
                two = w_ref[b + 1, pl.ds(a * 16, 16), :].astype(F32)
                at = pl.ds((a * plane + b) * 8, 16)
                wg_s[at, :] = jnp.concatenate([one[:8], two[:8]], axis=0).astype(BF16)
                wu_s[at, :] = jnp.concatenate([one[8:], two[8:]], axis=0).astype(BF16)
        for b in range(0, plane, 4):
            found = []
            for k in range(4):
                both = w_ref[b + k, pl.ds(16 * ring, 2 * padded), :].astype(F32)
                found.append(jnp.concatenate([both[:rows, :half], both[padded : padded + rows, :half]], axis=1))
            wd_s[pl.ds(b * rows, 4 * rows), :] = jnp.concatenate(found, axis=0).astype(BF16)

    x = x_ref[...]
    count = c_ref.shape[0] // ids_ref.shape[0]
    found = []
    for k in range(x.shape[0] // count):
        member = ids_ref[pl.program_id(0) * (x.shape[0] // count) + k]
        found.append(c_ref[pl.ds(pl.multiple_of(member * count, count), count), :])
    cotangent = jnp.concatenate(found, axis=0)
    gate_value = dot_nn(x, wg_s[...])
    upward = dot_nn(x, wu_s[...])
    grad_hidden = dot_nt(cotangent, wd_s[...])
    sigmoid = 1.0 / (1.0 + jnp.exp(-gate_value))
    silu = gate_value * sigmoid
    hidden = (silu * upward).astype(BF16)
    grad_gate = (grad_hidden * upward * sigmoid * (1.0 + gate_value * (1.0 - sigmoid))).astype(BF16)
    grad_up = (grad_hidden * silu).astype(BF16)
    h_ref[...] = hidden
    gg_ref[...] = grad_gate
    gu_ref[...] = grad_up
    parts_ref[...] = (dot_nt(grad_gate, wg_s[...]) + dot_nt(grad_up, wu_s[...])).astype(BF16)
    down_ref[...] = dot_nn(hidden, wd_s[...]).astype(BF16)


def feed_back_kernel(ids_ref, x_ref, h_ref, gg_ref, gu_ref, c_ref, raw_ref):
    plane, packed, ff = raw_ref.shape
    members = ids_ref.shape[0]
    total, width = c_ref.shape
    padded = (packed - 16 * members) // 2
    rows = ff // plane
    per = x_ref.shape[1] // (8 * plane)
    turned = transposed(x_ref[...]).astype(BF16)
    gate = dot_nn(turned, gg_ref[...]).reshape(per, plane, 8, ff)
    up = dot_nn(turned, gu_ref[...]).reshape(per, plane, 8, ff)
    for k in range(per):
        at = pl.multiple_of((pl.program_id(0) * per + k) * 16, 16)
        raw_ref[:, pl.ds(at, 16), :] = jnp.concatenate([gate[k], up[k]], axis=1).astype(BF16)

    @pl.when(pl.program_id(0) == 0)
    def _():
        count = total // members
        found = [c_ref[pl.ds(pl.multiple_of(ids_ref[k] * count, count), count), :] for k in range(members)]
        grad = dot_nn(transposed(h_ref[...]).astype(BF16), jnp.concatenate(found, axis=0))
        empty = jnp.zeros((padded - rows, ff), F32)
        beside = jnp.zeros((rows, ff - width // 2), F32)
        for b in range(plane):
            piece = grad[b * rows : (b + 1) * rows]
            stacked = []
            for k in range(2):
                part = piece[:, k * (width // 2) : (k + 1) * (width // 2)]
                stacked += [jnp.concatenate([part, beside], axis=1), empty]
            raw_ref[b, pl.ds(16 * members, 2 * padded), :] = jnp.concatenate(stacked, axis=0).astype(BF16)


def feed_forward(ids, feed, cotangent, weights):
    total, width = feed.shape
    plane, packed, ff = weights.shape
    steps = 2
    rows = total // steps
    row = lambda i, ids: (i, 0)
    return pl.pallas_call(
        feed_kernel,
        grid_spec=pltpu.PrefetchScalarGridSpec(
            num_scalar_prefetch=1,
            grid=(steps,),
            in_specs=[
                pl.BlockSpec((rows, width), row),
                pl.BlockSpec((total, width), lambda i, ids: (0, 0)),
                pl.BlockSpec((plane, packed, ff), lambda i, ids: (0, 0, 0)),
            ],
            out_specs=[pl.BlockSpec((rows, ff), row)] * 3 + [pl.BlockSpec((rows, width), row)] * 2,
            scratch_shapes=[pltpu.VMEM((width, ff), BF16), pltpu.VMEM((width, ff), BF16), pltpu.VMEM((ff, width), BF16)],
        ),
        out_shape=[jax.ShapeDtypeStruct((total, ff), BF16)] * 3 + [jax.ShapeDtypeStruct((total, width), BF16)] * 2,
        compiler_params=pltpu.CompilerParams(vmem_limit_bytes=40 * 2**20),
        cost_estimate=pl.CostEstimate(flops=8 * 10**9, bytes_accessed=15 * 10**6, transcendentals=10**6),
        name="feed_forward",
    )(ids, feed, cotangent, weights)


def feed_back(ids, feed, hidden, grad_gate, grad_up, cotangent, plane, packed):
    total, width = feed.shape
    ff = hidden.shape[1]
    steps = 2
    fixed = lambda i, ids: (0, 0)
    return pl.pallas_call(
        feed_back_kernel,
        grid_spec=pltpu.PrefetchScalarGridSpec(
            num_scalar_prefetch=1,
            grid=(steps,),
            in_specs=[
                pl.BlockSpec((total, width // steps), lambda i, ids: (0, i)),
                pl.BlockSpec((total, ff), fixed), pl.BlockSpec((total, ff), fixed), pl.BlockSpec((total, ff), fixed),
                pl.BlockSpec((total, width), fixed),
            ],
            out_specs=pl.BlockSpec((plane, packed, ff), lambda i, ids: (0, 0, 0)),
        ),
        out_shape=jax.ShapeDtypeStruct((plane, packed, ff), BF16),
        compiler_params=pltpu.CompilerParams(vmem_limit_bytes=48 * 2**20),
        cost_estimate=pl.CostEstimate(flops=4 * 10**9, bytes_accessed=12 * 10**6, transcendentals=0),
        name="feed_back",
    )(ids, feed, hidden, grad_gate, grad_up, cotangent)


def together(*values):
    return lax.optimization_barrier(values)


def ring_shift(values, axes, offset):
    return lax.ppermute(values, axes, [(i, (i - offset) % 4) for i in range(4)])


def other_core(values):
    return lax.ppermute(values, "c", [(0, 1), (1, 0)])


def near_ring(values):
    return [values] + [ring_shift(values, ("h", "l"), o) for o in OFFSETS[1:]]


def both_cores(near):
    near = jnp.concatenate(near, axis=0)
    return jnp.concatenate([near, other_core(near)], axis=0)


def gather_ring(values):
    return both_cores(near_ring(values))


def scatter_ring_first(parts):
    return (parts[:4].astype(F32) + other_core(parts[4:]).astype(F32)).astype(BF16)


def scatter_ring_second(mine):
    got = [ring_shift(mine[k], ("h", "l"), -OFFSETS[k]) for k in range(1, 4)]
    return [mine[0]] + got


def add_all(parts):
    total = parts[0].astype(F32)
    for part in parts[1:]:
        total = total + part.astype(F32)
    return total


def heads_to_tokens(values):
    parts = values.reshape(8, -1, values.shape[1])
    got = lax.all_to_all(parts, RING, split_axis=0, concat_axis=0, tiled=True)
    return got.transpose(1, 0, 2).reshape(parts.shape[1], -1)


def tokens_to_heads(values):
    parts = values.reshape(values.shape[0], 8, -1).transpose(1, 0, 2)
    got = lax.all_to_all(parts, RING, split_axis=0, concat_axis=0, tiled=True)
    return got.reshape(-1, parts.shape[2])


def gather_plane(values):
    half = values.shape[0] // 2
    first = [values[:half], values[half:]]
    lines = [[part] + [ring_shift(part, axis, o) for o in OFFSETS[1:]] for part, axis in zip(first, ("x", "z"))]
    lines = together(*[jnp.concatenate(line, axis=0) for line in lines])
    result = [[line] + [ring_shift(line, axis, o) for o in OFFSETS[1:]] for line, axis in zip(lines, ("z", "x"))]
    return result[0] + result[1]


def scatter_plane_first(pieces):
    parts = []
    for half, axis in ((pieces[:4], "z"), (pieces[4:], "x")):
        parts += [half[0]] + [ring_shift(half[k], axis, -OFFSETS[k]) for k in range(1, 4)]
    parts = together(*parts)
    return [add_all(parts[:4]).astype(BF16), add_all(parts[4:]).astype(BF16)]


def scatter_plane_second(lines):
    result = []
    for line, axis in zip(lines, ("x", "z")):
        part = line.reshape(4, -1, line.shape[1])
        result.append([part[0]] + [ring_shift(part[k], axis, -OFFSETS[k]) for k in range(1, 4)])
    return jnp.concatenate([add_all(parts) for parts in result], axis=0)


def rms(values):
    return lax.rsqrt(jnp.mean(values * values, axis=-1, keepdims=True) + EPS)


def rms_back(values, scale, upstream):
    inner = jnp.mean(values * upstream, axis=-1, keepdims=True)
    return scale * upstream - values * (scale * scale * scale) * inner


def to_all_plane(values):
    spread = jnp.broadcast_to(values[None], (16,) + values.shape)
    return lax.all_to_all(spread, PLANE, split_axis=0, concat_axis=0, tiled=True)


def sum_plane(parts):
    got = lax.all_to_all(parts.astype(BF16), PLANE, split_axis=0, concat_axis=0, tiled=True)
    return jnp.sum(got.astype(F32), axis=0)


def offset_of(slot):
    return jnp.where(slot == 1, -1, jnp.where(slot > 1, slot - 1, 0))


def places(span_order):
    me = lax.axis_index(AXES).astype(jnp.int32)
    number = jnp.arange(256, dtype=jnp.int32)
    device = me + jnp.zeros_like(number)
    half = number >> 7
    outer, inner = offset_of((number >> 5) & 3), offset_of((number >> 3) & 3)
    x = (((device >> 2) & 3) + jnp.where(half == 0, inner, outer)) & 3
    z = ((device & 3) + jnp.where(half == 0, outer, inner)) & 3
    member = half * 4 + ((number >> 1) & 3)
    span = 2 * (member * 16 + x * 4 + z) + (number & 1)
    streams = jnp.sum(jnp.where(span[:, None] == number[None, :], span_order[None, :], 0), axis=1)
    slots = jnp.sum(jnp.where(streams[None, :] == number[:, None], number[None, :], 0), axis=1)
    number = jnp.arange(8, dtype=jnp.int32)
    device = me + jnp.zeros_like(number)
    y = ((device >> 6) & 1) * 2 + ((device >> 4) & 1)
    y = (y + offset_of(number & 3)) & 3
    core = ((device >> 5) & 1) ^ (number >> 2)
    return streams, slots, (y >> 1) * 4 + core * 2 + (y & 1)


def rotary_tables(blocks, starts):
    stream = (blocks[:, None] * SPAN + jnp.arange(SPAN, dtype=jnp.int32)[None, :]).reshape(-1, 1)
    begins = jnp.zeros_like(stream)
    for number in range(1, SEQS):
        begins = jnp.where(stream >= starts[number], starts[number], begins)
    inverse = jnp.power(THETA, -jnp.arange(0, HEAD_DIM, 2).astype(F32) / HEAD_DIM)
    angles = (stream - begins).astype(F32) * jnp.tile(inverse, 4)[None, :]
    return jnp.cos(angles), jnp.sin(angles)


def local(
    tokens, document_ids, span_order, attention_gain, head_gain, qkv_weight, out_weight,
    feed_gain, gate_weight, up_weight, down_weight, cotangent,
):
    rows, width = tokens.shape
    ring, plane = 8, 16
    down_rows = down_weight.shape[0]
    ff = down_rows * plane
    half = width // 2
    pad_rows, pad_columns = -down_rows % 8, ff - half
    near_tokens = near_ring(tokens)
    ring_cotangent = lax.all_gather(cotangent, RING, axis=0, tiled=True)

    gain_a = attention_gain.astype(F32)[:, None]
    gain_f = feed_gain.astype(F32)[:, None]
    scaled_qkv = (gain_a * qkv_weight.astype(F32)).astype(BF16)
    qw, kw, vw = scaled_qkv[:, :1024], scaled_qkv[:, 1024:1536], scaled_qkv[:, 1536:]
    by_head = jnp.concatenate(
        [v.reshape(8, ring, -1).transpose(1, 0, 2) for v in (qw, kw, vw)], axis=2
    )
    gain_rows = jnp.broadcast_to(head_gain.reshape(1, 1, 1), (ring, 8, by_head.shape[2]))
    message = jnp.concatenate([by_head, gain_rows], axis=1)
    message = jnp.pad(message, ((0, 0), (0, 0), (0, ff - message.shape[2])))
    gate_up = jnp.stack([gate_weight, up_weight])
    scaled_gate_up = (gain_f * gate_up.astype(F32)).astype(BF16)
    feed_message = scaled_gate_up.reshape(2, 8, ring, ff).transpose(2, 0, 1, 3).reshape(ring, 16, ff)
    message = jnp.concatenate([message, feed_message], axis=1)
    message = lax.all_to_all(message, RING, split_axis=0, concat_axis=0, tiled=True)
    message, *near_tokens = together(message, *near_tokens)
    ring_tokens = both_cores(near_tokens)
    feed_message = message[:, 16:]
    message = message[:, :16, :256]
    head_gains = jnp.broadcast_to(message[:, 8, :1], (ring, 256))
    out_rows = out_weight.reshape(8, 4, 256).transpose(1, 0, 2).reshape(32, 256)
    message = jnp.concatenate([message[:, :8].reshape(ring * 8, -1), head_gains, out_rows], axis=0)
    gathered = to_all_plane(message)
    own_qkv = gathered[:, :64].reshape(plane, ring, 8, -1).transpose(1, 0, 2, 3).reshape(width, -1)
    gains = gathered[:, 64:72, 0].T.reshape(1, 2 * HEAD_DIM).astype(F32)
    gains = jnp.concatenate([gains[:, :HEAD_DIM], gains, jnp.ones((1, HEAD_DIM), F32)], axis=1)
    own_out = gathered[:, 72:].reshape(plane, 4, 8, 256).transpose(0, 2, 1, 3).reshape(8 * plane, width)
    all_out = lax.all_gather(own_out, RING, axis=0, tiled=True)

    starts = jnp.sum(
        (document_ids[None, :] < jnp.arange(SEQS, dtype=jnp.int32)[:, None]).astype(jnp.int32), axis=1
    )
    streams, slots, ring_ids = places(span_order)
    own_blocks = jnp.concatenate([streams[:8], streams[128:136]])
    cosine, sine = rotary_tables(own_blocks, starts)
    items, tiles, groups = work_list(own_blocks, starts, document_ids.shape[0])
    tables = (streams, slots, items, tiles, groups, starts)

    ring_normed, projected, queries, key_values = project(ring_ids, ring_tokens, own_qkv, cosine, sine, gains)
    all_kv = gather_plane(key_values)
    down_halves = jnp.stack([down_weight[:, :half], down_weight[:, half:]])
    down_halves = jnp.pad(down_halves, ((0, 0), (0, pad_rows), (0, pad_columns)))
    message = jnp.concatenate([feed_message.reshape(ring * 16, ff), down_halves.reshape(-1, ff)], axis=0)
    *all_kv, message = together(*all_kv, message)
    feed_weights = lax.all_gather(message, PLANE, axis=0, tiled=True).reshape(plane, -1, ff)
    outputs, attended, logs = attention_forward(tables, queries, all_kv)
    head_outputs = heads_to_tokens(attended)
    residual = tokens.astype(F32) + dot_nn(head_outputs, all_out)
    feed_scale = rms(residual)
    ring_feed = gather_ring((residual * feed_scale).astype(BF16))
    hidden, grad_gate, grad_up, feed_parts, down_parts = feed_forward(
        ring_ids, ring_feed, ring_cotangent, feed_weights
    )

    mine = scatter_ring_first(feed_parts.reshape(ring, rows, width))
    mine, hidden, down_parts = together(mine, hidden, down_parts)
    grad_feed = scatter_ring_second(mine)
    raw = feed_back(ring_ids, ring_feed, hidden, grad_gate, grad_up, ring_cotangent, plane, message.shape[0])
    mine_down = scatter_ring_first(down_parts.reshape(ring, rows, width))
    *grad_feed, raw, mine_down = together(*grad_feed, raw, mine_down)
    raw = lax.psum_scatter(raw.reshape(-1, ff), PLANE, scatter_dimension=0, tiled=True)
    grad_residual = cotangent.astype(F32) + rms_back(residual, feed_scale, add_all(grad_feed))
    grad_attended = grad_residual.astype(BF16)
    grad_heads = tokens_to_heads(dot_nt(grad_attended, all_out).astype(BF16))
    grad_heads, mine_down, late_attended = together(grad_heads, mine_down, grad_attended)
    output_parts = scatter_ring_second(mine_down)
    near_attended = near_ring(late_attended)

    grad_queries, *grad_kv_parts = attention_backward(
        tables, queries, grad_heads, outputs, logs, all_kv
    )
    count = len(output_parts)
    others = together(*grad_kv_parts, *output_parts, *near_attended)
    lines = scatter_plane_first(others[:PIECES])
    others = others[PIECES:]
    one, two, *others = together(*lines, *others)
    grad_kv = scatter_plane_second([one, two])
    block_output = (residual + add_all(others[:count])).astype(BF16)
    near = others[count:]
    grad_out = out_back(ring_ids, attended, near, other_core(jnp.concatenate(near, axis=0)))
    grad_kv, block_output, grad_out, raw = together(grad_kv, block_output, grad_out, raw)
    grad_projected, norm_parts, grad_gains = project_back(
        ring_ids, grad_queries, grad_kv, projected, cosine, sine, gains, own_qkv
    )
    mine = scatter_ring_first(norm_parts.reshape(ring, rows, width))

    back = dot_tn(ring_normed, grad_projected).astype(BF16)
    back = back.reshape(ring, plane, 8, -1).transpose(1, 0, 2, 3).reshape(plane, ring * 8, -1)
    grad_gains = jnp.sum(grad_gains, axis=0)
    grad_gains = jnp.concatenate([grad_gains[:64] + grad_gains[64:128], grad_gains[128:192]])
    gain_part = grad_gains.reshape(ring, plane).T.reshape(plane, ring, 1).astype(BF16)
    gain_part = jnp.broadcast_to(gain_part, (plane, ring, 256))
    grad_out = grad_out.reshape(plane, 8, 4, 256).transpose(0, 2, 1, 3).reshape(plane, 32, 256)
    back = jnp.concatenate([back, gain_part, grad_out], axis=1)
    mine, back = together(mine, back)
    grad_norm = scatter_ring_second(mine)
    back = sum_plane(back)
    *grad_norm, back = together(*grad_norm, back)
    own_tokens = tokens.astype(F32)
    grad_tokens = grad_residual + rms_back(own_tokens, rms(own_tokens), add_all(grad_norm))
    grad_out = back[72:].reshape(4, 8, 256).transpose(1, 0, 2).reshape(8, width)
    gain_part = jnp.broadcast_to(back[64:72, None], (ring, 8, 256))
    back = jnp.concatenate([back[:64].reshape(ring, 8, 256), gain_part], axis=1).astype(BF16)
    back = jnp.pad(back, ((0, 0), (0, 0), (0, ff - back.shape[2])))
    back = jnp.concatenate([back, raw[: ring * 16].reshape(ring, 16, ff)], axis=1)
    back = lax.all_to_all(back, RING, split_axis=0, concat_axis=0, tiled=True).astype(F32)
    back, raw_back = back[:, :16, :256], back[:, 16:]
    grad_head_gain = jnp.sum(back[:, 8, 0]).reshape(1)
    back = back[:, :8].transpose(1, 0, 2)
    back = jnp.concatenate(
        [back[:, :, lo:hi].reshape(8, -1) for lo, hi in ((0, 128), (128, 192), (192, 256))], axis=1
    )
    grad_qkv_weight = gain_a * back
    grad_attention_gain = jnp.sum(back * qkv_weight.astype(F32), axis=1)

    raw_down = raw[ring * 16 :].reshape(2, -1, ff)[:, :down_rows, :half]
    grad_down = jnp.concatenate([raw_down[0], raw_down[1]], axis=1).astype(F32)
    raw = raw_back.reshape(ring, 2, 8, ff).transpose(1, 2, 0, 3).reshape(2, 8, ring * ff)
    grad_gate_weight, grad_up_weight = gain_f * raw[0], gain_f * raw[1]
    grad_feed_gain = jnp.sum(raw * gate_up.astype(F32), axis=(0, 2))
    return (
        block_output, grad_tokens, grad_attention_gain, grad_head_gain, grad_qkv_weight, grad_out,
        grad_feed_gain, grad_gate_weight, grad_up_weight, grad_down,
    )


def solution(mesh):
    fine = Mesh(mesh.devices.reshape(2, 2, 2, 4, 4), AXES)
    one, two, whole = P(AXES), P(AXES, None), P()
    in_specs = (two, whole, whole, one, one, two, two, one, two, two, two, two)
    out_specs = (two, two, one, one, two, two, one, two, two, two)
    return jax.shard_map(local, mesh=fine, in_specs=in_specs, out_specs=out_specs, check_vma=False)
```

```python
import functools

import jax
import jax.numpy as jnp
from jax import lax
from jax.experimental import pallas as pl
from jax.experimental.pallas import tpu as pltpu
from jax.sharding import Mesh
from jax.sharding import PartitionSpec as P

F32 = jnp.float32
BF16 = jnp.bfloat16
HEADS = 16
KV_HEADS = 8
HEAD_DIM = 64
SEQS = 4
SPAN = 64
EPS = 1e-05
THETA = 1000000.0
LOG2E = 1.4426950408889634
LN2 = 0.6931471805599453
SCORE_SCALE = HEAD_DIM ** -0.5

AXES = ("h", "c", "l", "x", "z")
RING = ("h", "c", "l")
PLANE = ("x", "z")
OFFSETS = (0, -1, 1, 2)

TILE, PAIR, PIECES = 1024, 2, 8
FORWARD_UNROLL, BACKWARD_UNROLL = 4, 4
PAIR_ROWS = 2 * SPAN


def dot_nn(left, right):
    return lax.dot_general(left, right, (((1,), (0,)), ((), ())), preferred_element_type=F32)


def dot_nt(left, right):
    return lax.dot_general(left, right, (((1,), (1,)), ((), ())), preferred_element_type=F32)


def dot_tn(left, right):
    return lax.dot_general(left, right, (((0,), (0,)), ((), ())), preferred_element_type=F32)


def transposed(values):
    return values.astype(F32).T


def heads_beside(block):
    turned = transposed(block)
    return jnp.concatenate([turned[:HEAD_DIM], turned[HEAD_DIM:]], axis=1)


def heads_back(turned):
    return jnp.concatenate([turned[:, :SPAN], turned[:, SPAN:]], axis=0).T


def fetch(pieces, raw_s, sem):
    rows = pieces[0].shape[0]
    return [
        pltpu.make_async_copy(piece, raw_s.at[pl.ds(k * rows, rows)], sem.at[k]) for k, piece in enumerate(pieces)
    ]


def sort_keys(raw_s, stream_ref, kv_s, kvt_s):
    per = 8

    def place(group, carry):
        for u in range(per):
            block = group * per + u
            target = pl.multiple_of(stream_ref[block] * SPAN, SPAN)
            kv_s[pl.ds(target, SPAN), :] = raw_s[pl.ds(pl.multiple_of(block * SPAN, SPAN), SPAN), :]
        return carry

    lax.fori_loop(0, raw_s.shape[0] // SPAN // per, place, 0)

    def turn(block, carry):
        first = pl.multiple_of(block * TILE, TILE)
        kvt_s[:, pl.ds(first, TILE)] = transposed(kv_s[pl.ds(first, TILE), :]).astype(BF16)
        return carry

    lax.fori_loop(0, kv_s.shape[0] // TILE, turn, 0)


def row_limits(blocks, stream_ref, starts_ref, limit_s):
    half = stream_ref.shape[0] // 2
    for i in range(blocks):
        block = stream_ref[i if i < blocks // 2 else half + i - blocks // 2]
        position = block * SPAN + (lax.broadcasted_iota(jnp.int32, (1, PAIR_ROWS), 1) & (SPAN - 1))
        begin = jnp.zeros((1, PAIR_ROWS), jnp.int32)
        for number in range(1, SEQS):
            begin = jnp.where(position >= starts_ref[number], starts_ref[number], begin)
        limit_s[i, 0:1] = begin
        limit_s[i, 1:2] = position
    limit_s[blocks, 0:1] = jnp.ones((1, PAIR_ROWS), jnp.int32)
    limit_s[blocks, 1:2] = jnp.zeros((1, PAIR_ROWS), jnp.int32)


def visible(item, first, limit_s):
    key = lax.broadcasted_iota(jnp.int32, (TILE, PAIR_ROWS), 0)
    return (key >= limit_s[item, 0:1] - first) & (key <= limit_s[item, 1:2] - first)


def all_groups(some, count_ref, unroll):
    first = jnp.int32(0)
    for kind in range(2):
        whole = lax.div(count_ref[kind] - first, unroll)

        def several(step, carry, first=first, kind=kind):
            some([first + step * unroll + u for u in range(unroll)], kind == 1)
            return carry

        def one(at, carry, kind=kind):
            some([at], kind == 1)
            return carry

        lax.fori_loop(0, whole, several, 0)
        lax.fori_loop(first + whole * unroll, count_ref[kind], one, 0)
        first = count_ref[kind]


def forward_kernel(stream_ref, item_ref, tile_ref, count_ref, starts_ref, q_ref, *refs):
    pieces = refs[:PIECES]
    _, o_ref, low_ref, l_ref, raw_s, kv_s, kvt_s, qt_s, acc_s, sum_s, limit_s, sem = refs[PIECES:]
    blocks = q_ref.shape[0] // SPAN
    copies = fetch(pieces, raw_s, sem)
    for copy in copies:
        copy.start()
    for i in range(blocks):
        qt_s[i, :HEAD_DIM] = heads_beside(q_ref[pl.ds(i * SPAN, SPAN), :]).astype(BF16)
        qt_s[i, HEAD_DIM:] = jnp.zeros((HEAD_DIM, PAIR_ROWS), BF16)
    qt_s[blocks] = jnp.zeros((2 * HEAD_DIM, PAIR_ROWS), BF16)
    row_limits(blocks, stream_ref, starts_ref, limit_s)
    acc_s[...] = jnp.zeros(acc_s.shape, F32)
    sum_s[...] = jnp.zeros(sum_s.shape, F32)
    for copy in copies:
        copy.wait()
    sort_keys(raw_s, stream_ref, kv_s, kvt_s)

    def some(groups, masked):
        found = []
        for at in groups:
            items = [item_ref[at * PAIR + k] for k in range(PAIR)]
            first = pl.multiple_of(tile_ref[at] * TILE, TILE)
            right = jnp.concatenate([qt_s[i] for i in items], axis=1)
            weights = jnp.exp2(dot_nn(kv_s[pl.ds(first, TILE), :], right))
            if masked:
                seen = jnp.concatenate([visible(i, first, limit_s) for i in items], axis=1)
                weights = jnp.where(seen, weights, 0.0)
            update = dot_nn(kvt_s[HEAD_DIM:, pl.ds(first, TILE)], weights.astype(BF16))
            part = jnp.sum(weights.reshape(TILE // 8, 8, PAIR * PAIR_ROWS), axis=0)
            found.append((items, update, part))
        for items, update, part in found:
            for k, i in enumerate(items):
                at = slice(k * PAIR_ROWS, (k + 1) * PAIR_ROWS)
                acc_s[i] += update[:, at]
                sum_s[i] += part[:, at]

    all_groups(some, count_ref, FORWARD_UNROLL)
    for i in range(blocks):
        total = jnp.sum(sum_s[i], axis=0, keepdims=True)
        result = heads_back(acc_s[i] * (1.0 / total))
        o_ref[pl.ds(i * SPAN, SPAN), :] = result
        low_ref[pl.ds(i * SPAN, SPAN), :] = result.astype(BF16)
        l_ref[i] = jnp.broadcast_to(jnp.log2(total), (8, PAIR_ROWS))


def backward_kernel(
    stream_ref, item_ref, tile_ref, count_ref, starts_ref, q_ref, do_ref, o_ref, l_ref, *refs
):
    pieces, dq_ref, outs = refs[:PIECES], refs[PIECES], refs[PIECES + 1 : 2 * PIECES + 1]
    raw_s, kv_s, kvt_s, left_s, right_s, stat_s, limit_s, dq_s, dkv_s, sem = refs[2 * PIECES + 1 :]
    blocks = q_ref.shape[0] // SPAN
    copies = fetch(pieces, raw_s, sem)
    for copy in copies:
        copy.start()
    nothing = jnp.zeros((HEAD_DIM, PAIR_ROWS), F32)
    for i in range(blocks):
        rows = pl.ds(i * SPAN, SPAN)
        grad_out = heads_beside(do_ref[rows, :])
        query_side = jnp.concatenate([heads_beside(q_ref[rows, :]), nothing], axis=0)
        grad_side = jnp.concatenate([nothing, grad_out], axis=0)
        right_s[i, :, :PAIR_ROWS] = query_side.astype(BF16)
        right_s[i, :, PAIR_ROWS:] = grad_side.astype(BF16)
        left_s[i, :PAIR_ROWS] = query_side.T.astype(BF16)
        left_s[i, PAIR_ROWS:] = grad_side.T.astype(BF16)
        stat_s[i, 0:1] = l_ref[i][0:1]
        stat_s[i, 1:2] = jnp.sum(grad_out * heads_beside(o_ref[rows, :]), axis=0, keepdims=True)
    left_s[blocks] = jnp.zeros(left_s.shape[1:], BF16)
    right_s[blocks] = jnp.zeros(right_s.shape[1:], BF16)
    stat_s[blocks] = jnp.zeros(stat_s.shape[1:], F32)
    row_limits(blocks, stream_ref, starts_ref, limit_s)
    dq_s[...] = jnp.zeros(dq_s.shape, F32)

    def clear(block, carry):
        dkv_s[pl.ds(pl.multiple_of(block * TILE, TILE), TILE), :] = jnp.zeros((TILE, 2 * HEAD_DIM), F32)
        return carry

    lax.fori_loop(0, kv_s.shape[0] // TILE, clear, 0)
    for copy in copies:
        copy.wait()
    sort_keys(raw_s, stream_ref, kv_s, kvt_s)

    def some(groups, masked):
        found = []
        for at in groups:
            items = [item_ref[at * PAIR + k] for k in range(PAIR)]
            first = pl.multiple_of(tile_ref[at] * TILE, TILE)
            keys = kv_s[pl.ds(first, TILE), :]
            mixed, grads = [], []
            for i in items:
                both = dot_nn(keys, right_s[i])
                weights = jnp.exp2(both[:, :PAIR_ROWS] - stat_s[i, 0:1])
                if masked:
                    weights = jnp.where(visible(i, first, limit_s), weights, 0.0)
                grad = (weights * (both[:, PAIR_ROWS:] - stat_s[i, 1:2])).astype(BF16)
                grads.append(grad)
                mixed += [grad, weights.astype(BF16)]
            update = dot_nn(kvt_s[:HEAD_DIM, pl.ds(first, TILE)], jnp.concatenate(grads, axis=1))
            left = jnp.concatenate([left_s[i] for i in items], axis=0)
            found.append((items, first, update, dot_nn(jnp.concatenate(mixed, axis=1), left)))
        for items, first, update, fresh in found:
            for k, i in enumerate(items):
                dq_s[i] += update[:, k * PAIR_ROWS : (k + 1) * PAIR_ROWS]
            dkv_s[pl.ds(first, TILE), :] += fresh

    all_groups(some, count_ref, BACKWARD_UNROLL)
    for i in range(blocks):
        dq_ref[pl.ds(i * SPAN, SPAN), :] = heads_back(dq_s[i]) * SCORE_SCALE
    lane = lax.broadcasted_iota(jnp.int32, (1, 2 * HEAD_DIM), 1)
    scale = jnp.where(lane < HEAD_DIM, LN2, 1.0)
    rows = outs[0].shape[0]
    for k, out in enumerate(outs):

        def one(group, carry, k=k, out=out):
            for u in range(8):
                block = group * 8 + u
                source = pl.multiple_of(stream_ref[k * (rows // SPAN) + block] * SPAN, SPAN)
                target = pl.multiple_of(block * SPAN, SPAN)
                out[pl.ds(target, SPAN), :] = (dkv_s[pl.ds(source, SPAN), :] * scale).astype(BF16)
            return carry

        lax.fori_loop(0, rows // SPAN // 8, one, 0)


IN_VMEM = pl.BlockSpec(memory_space=pltpu.VMEM)
ANYWHERE = pl.BlockSpec(memory_space=pl.ANY)
IN_HBM = pl.BlockSpec(memory_space=pltpu.HBM)


def attention_forward(tables, queries, pieces, before):
    rows, part = queries.shape[0], pieces[0].shape[0]
    blocks, total = rows // SPAN, PIECES * part
    return pl.pallas_call(
        forward_kernel,
        grid_spec=pltpu.PrefetchScalarGridSpec(
            num_scalar_prefetch=5,
            grid=(),
            in_specs=[IN_VMEM] + [IN_HBM] * PIECES + [ANYWHERE],
            out_specs=[IN_VMEM] * 3,
            scratch_shapes=[
                pltpu.VMEM((total, 128), BF16),
                pltpu.VMEM((total, 128), BF16),
                pltpu.VMEM((128, total), BF16),
                pltpu.VMEM((blocks + 1, 128, 128), BF16),
                pltpu.VMEM((blocks + 1, HEAD_DIM, 128), F32),
                pltpu.VMEM((blocks + 1, 8, 128), F32),
                pltpu.VMEM((blocks + 1, 8, 128), jnp.int32),
                pltpu.SemaphoreType.DMA((PIECES,)),
            ],
        ),
        out_shape=[
            jax.ShapeDtypeStruct((rows, 128), F32),
            jax.ShapeDtypeStruct((rows, 128), BF16),
            jax.ShapeDtypeStruct((blocks, 8, 128), F32),
        ],
        compiler_params=pltpu.CompilerParams(vmem_limit_bytes=60 * 2**20),
        cost_estimate=pl.CostEstimate(flops=20 * 10**9, bytes_accessed=6 * 10**6, transcendentals=10**7),
        name="attention_forward",
    )(*tables, queries, *pieces, before)


def attention_backward(tables, queries, grad_out, outputs, logs, pieces):
    rows, part = queries.shape[0], pieces[0].shape[0]
    blocks, total = rows // SPAN, PIECES * part
    return pl.pallas_call(
        backward_kernel,
        grid_spec=pltpu.PrefetchScalarGridSpec(
            num_scalar_prefetch=5,
            grid=(),
            in_specs=[IN_VMEM] * 4 + [IN_HBM] * PIECES,
            out_specs=[IN_VMEM] * (1 + PIECES),
            scratch_shapes=[
                pltpu.VMEM((total, 128), BF16),
                pltpu.VMEM((total, 128), BF16),
                pltpu.VMEM((128, total), BF16),
                pltpu.VMEM((blocks + 1, 256, 128), BF16),
                pltpu.VMEM((blocks + 1, 128, 256), BF16),
                pltpu.VMEM((blocks + 1, 8, 128), F32),
                pltpu.VMEM((blocks + 1, 8, 128), jnp.int32),
                pltpu.VMEM((blocks + 1, HEAD_DIM, 128), F32),
                pltpu.VMEM((total, 128), F32),
                pltpu.SemaphoreType.DMA((PIECES,)),
            ],
        ),
        out_shape=[jax.ShapeDtypeStruct((rows, 128), F32)] + [jax.ShapeDtypeStruct((part, 128), BF16)] * PIECES,
        compiler_params=pltpu.CompilerParams(vmem_limit_bytes=60 * 2**20),
        cost_estimate=pl.CostEstimate(flops=40 * 10**9, bytes_accessed=10**7, transcendentals=10**7),
        name="attention_backward",
    )(*tables, queries, grad_out, outputs, logs, *pieces)


def work_list(blocks, starts, total):
    count, tiles = blocks.shape[0], total // TILE
    first = blocks * SPAN
    begin, begin_last = jnp.zeros_like(first), jnp.zeros_like(first)
    for number in range(1, SEQS):
        begin = jnp.where(first >= starts[number], starts[number], begin)
        begin_last = jnp.where(first + (SPAN - 1) >= starts[number], starts[number], begin_last)
    shift = TILE.bit_length() - 1
    number = jnp.arange(tiles, dtype=jnp.int32)
    active = (number[:, None] >= (begin >> shift)[None, :]) & (number[:, None] <= (first >> shift)[None, :])
    low = number[:, None] * TILE
    full = active & (low >= begin_last[None, :]) & (low + (TILE - 1) <= first[None, :])
    index = jnp.arange(count, dtype=jnp.int32)
    before = (index[:, None] < index[None, :]).astype(jnp.int32)
    is_full, is_part = full.astype(jnp.int32), (active & ~full).astype(jnp.int32)
    count_full, count_part = jnp.sum(is_full, axis=1), jnp.sum(is_part, axis=1)
    rank_full = jnp.sum(is_full[:, :, None] * before[None], axis=1)
    rank_part = jnp.sum(is_part[:, :, None] * before[None], axis=1) + count_full[:, None]
    rank = jnp.where(full, rank_full, jnp.where(active, rank_part, -1))
    half = PAIR.bit_length() - 1
    free = count_full >> half
    masked = ((count_full + count_part + (PAIR - 1)) >> half) - free
    counts = jnp.concatenate([free, masked])
    offset = jnp.concatenate([jnp.zeros_like(free), free * PAIR])
    place = jnp.arange(2 * tiles, dtype=jnp.int32)
    upto = (place[:, None] <= place[None, :]).astype(jnp.int32)
    ends = jnp.sum(counts[:, None] * upto, axis=0)
    group = jnp.arange(tiles * (count // PAIR), dtype=jnp.int32)
    past = group[:, None] >= ends[None, :]
    which = jnp.sum(past.astype(jnp.int32), axis=1)
    base = jnp.sum(jnp.where(past, counts[None, :], 0), axis=1)
    mine = which[:, None] == place[None, :]
    skip = jnp.sum(jnp.where(mine, offset[None, :], 0), axis=1)
    tile = which & (tiles - 1)
    ranks = jnp.sum(jnp.where((tile[:, None] == number[None, :])[:, :, None], rank[None] + 1, 0), axis=1) - 1
    want = ((group - base) * PAIR + skip)[:, None] + jnp.arange(PAIR, dtype=jnp.int32)[None, :]
    hit = ranks[:, None, :] == want[:, :, None]
    item = count - jnp.sum(jnp.where(hit, (count - index)[None, None, :], 0), axis=2)
    return item.reshape(-1), tile, ends[tiles - 1 :: tiles]


def rotated(values):
    lane = lax.broadcasted_iota(jnp.int32, values.shape, 1)
    up = pltpu.roll(values, 32, 1)
    down = pltpu.roll(values, 96, 1)
    return jnp.where((lane & 63) < 32, -down, up)


def head_mean(values):
    size = values.shape[1]
    row = lax.broadcasted_iota(jnp.int32, (size, size), 0)
    column = lax.broadcasted_iota(jnp.int32, (size, size), 1)
    same = jnp.where((row >> 6) == (column >> 6), 1.0 / HEAD_DIM, 0.0).astype(BF16)
    high = values.astype(BF16)
    low = (values - high.astype(F32)).astype(BF16)
    return dot_nn(high, same) + dot_nn(low, same)


def slot_rows(near, far_ref, slot):
    rows = near[0].shape[0]
    return near[slot][...] if slot < len(near) else far_ref[(slot - len(near)) * rows : (slot - len(near) + 1) * rows, :]


def project_kernel(ids_ref, *refs):
    *near, far_ref, w_ref, cos_ref, sin_ref, gain_ref, _, n_ref, p_ref, q_ref, kv_ref = refs
    rows = near[0].shape[0]
    for slot in range(0, 2 * len(near), 2):
        places = [pl.ds(pl.multiple_of(ids_ref[slot + k] * rows, rows), rows) for k in range(2)]
        values = jnp.concatenate([slot_rows(near, far_ref, slot + k) for k in range(2)], axis=0).astype(F32)
        normed = (values * lax.rsqrt(jnp.mean(values * values, axis=1, keepdims=True) + EPS)).astype(BF16)
        projected = dot_nn(normed, w_ref[...])
        heads = projected * lax.rsqrt(head_mean(projected * projected) + EPS) * gain_ref[...]
        cosine = jnp.concatenate([cos_ref[at, :] for at in places], axis=0)
        sine = jnp.concatenate([sin_ref[at, :] for at in places], axis=0)
        query, key = heads[:, :128], heads[:, 128:]
        query = (query * cosine + rotated(query) * sine) * (SCORE_SCALE * LOG2E)
        key = key * cosine + rotated(key) * sine
        lane = lax.broadcasted_iota(jnp.int32, key.shape, 1)
        key = jnp.where(lane < HEAD_DIM, key, projected[:, 128:])
        for k, at in enumerate(places):
            mine = slice(k * rows, (k + 1) * rows)
            n_ref[at, :] = normed[mine]
            p_ref[at, :] = projected[mine]
            q_ref[at, :] = query[mine].astype(BF16)
            kv_ref[at, :] = key[mine].astype(BF16)


def project_back_kernel(ids_ref, dq_ref, dkv_ref, p_ref, cos_ref, sin_ref, gain_ref, w_ref, gp_ref, parts_ref, gg_ref):
    rows = cos_ref.shape[0] // ids_ref.shape[0]
    count = parts_ref.shape[0] // rows
    places = []
    for k in range(count):
        member = ids_ref[pl.program_id(0) * count + k]
        places.append(pl.ds(pl.multiple_of(member * rows, rows), rows))

    def read(ref):
        return jnp.concatenate([ref[at, :] for at in places], axis=0)

    cosine, sine, values = read(cos_ref), read(sin_ref), read(p_ref)
    query = read(dq_ref).astype(BF16).astype(F32)
    key = read(dkv_ref).astype(BF16).astype(F32)
    upstream = jnp.concatenate(
        [query * cosine - rotated(query) * sine, key * cosine - rotated(key) * sine], axis=1
    )
    scale = lax.rsqrt(head_mean(values * values) + EPS)
    weighted = upstream * gain_ref[...]
    inner = head_mean(values * weighted)
    back = scale * weighted - values * (scale * scale * scale) * inner
    lane = lax.broadcasted_iota(jnp.int32, key.shape, 1)
    back = jnp.concatenate([back[:, :128], jnp.where(lane < HEAD_DIM, back[:, 128:], key)], axis=1)
    back = back.astype(BF16)
    for k, at in enumerate(places):
        gp_ref[at, :] = back[k * rows : (k + 1) * rows]
    parts_ref[...] = dot_nt(back, w_ref[...]).astype(BF16)

    @pl.when(pl.program_id(0) == 0)
    def _():
        gg_ref[...] = jnp.zeros(gg_ref.shape, F32)

    terms = upstream * values * scale
    gg_ref[...] += jnp.sum(terms.reshape(-1, 8, terms.shape[1]), axis=0)


def by_slot(rows, width):
    return pl.BlockSpec((rows, width), lambda i, ids: (i, 0))


def whole_block(shape):
    return pl.BlockSpec(shape, lambda i, ids: (0, 0))


def project(ids, near, far, weight, cosine, sine, gains, before):
    width = far.shape[1]
    total = 2 * far.shape[0]
    return pl.pallas_call(
        project_kernel,
        in_specs=[pl.BlockSpec(memory_space=pltpu.SMEM)] + [IN_VMEM] * (5 + len(near)) + [ANYWHERE],
        out_specs=[IN_VMEM] * 4,
        out_shape=[
            jax.ShapeDtypeStruct((total, width), BF16),
            jax.ShapeDtypeStruct((total, 256), F32),
            jax.ShapeDtypeStruct((total, 128), BF16),
            jax.ShapeDtypeStruct((total, 128), BF16),
        ],
        compiler_params=pltpu.CompilerParams(vmem_limit_bytes=24 * 2**20),
        cost_estimate=pl.CostEstimate(flops=10**9, bytes_accessed=8 * 10**6, transcendentals=10**5),
        name="project",
    )(ids, *near, far, weight, cosine, sine, gains, before)


def project_back(ids, grad_q, grad_kv, projected, cosine, sine, gains, weight):
    total, width = grad_q.shape[0], weight.shape[0]
    steps = ids.shape[0] // 2
    return pl.pallas_call(
        project_back_kernel,
        grid_spec=pltpu.PrefetchScalarGridSpec(
            num_scalar_prefetch=1,
            grid=(steps,),
            in_specs=[whole_block((total, wide)) for wide in (128, 128, 256, 128, 128)]
            + [whole_block((1, 256)), whole_block(weight.shape)],
            out_specs=[whole_block((total, 256)), by_slot(total // steps, width), whole_block((8, 256))],
        ),
        out_shape=[
            jax.ShapeDtypeStruct((total, 256), BF16),
            jax.ShapeDtypeStruct((total, width), BF16),
            jax.ShapeDtypeStruct((8, 256), F32),
        ],
        compiler_params=pltpu.CompilerParams(vmem_limit_bytes=24 * 2**20),
        cost_estimate=pl.CostEstimate(flops=10**9, bytes_accessed=8 * 10**6, transcendentals=10**5),
        name="project_back",
    )(ids, grad_q, grad_kv, projected, cosine, sine, gains, weight)


def out_back_kernel(ids_ref, a_ref, *refs):
    *near, far_ref, out_ref = refs
    rows = near[0].shape[0]
    total = jnp.zeros(out_ref.shape, F32)
    for k in range(2 * len(near)):
        block = near[k][...] if k < len(near) else far_ref[pl.ds((k - len(near)) * rows, rows), :]
        mine = a_ref[pl.ds(pl.multiple_of(ids_ref[k] * rows, rows), rows), :]
        total += dot_nn(transposed(mine).astype(BF16), block)
    out_ref[...] = total.astype(BF16)


def out_back(ids, attended, near, far):
    return pl.pallas_call(
        out_back_kernel,
        in_specs=[pl.BlockSpec(memory_space=pltpu.SMEM)] + [IN_VMEM] * (2 + len(near)),
        out_specs=IN_VMEM,
        out_shape=jax.ShapeDtypeStruct((attended.shape[1], far.shape[1]), BF16),
        compiler_params=pltpu.CompilerParams(vmem_limit_bytes=16 * 2**20),
        cost_estimate=pl.CostEstimate(flops=3 * 10**8, bytes_accessed=3 * 10**6, transcendentals=0),
        name="out_back",
    )(ids, attended, *near, far)


def unpack_kernel(w_ref, _, wg_ref, wu_ref, wd_ref):
    plane, packed, ff = w_ref.shape
    width = wg_ref.shape[0]
    ring = width // (8 * plane)
    rows = wd_ref.shape[0] // plane
    half = width // 2
    padded = (packed - 16 * ring) // 2
    for a in range(ring):
        for b in range(0, plane, 2):
            one = w_ref[b, pl.ds(a * 16, 16), :].astype(F32)
            two = w_ref[b + 1, pl.ds(a * 16, 16), :].astype(F32)
            at = pl.ds((a * plane + b) * 8, 16)
            wg_ref[at, :] = jnp.concatenate([one[:8], two[:8]], axis=0).astype(BF16)
            wu_ref[at, :] = jnp.concatenate([one[8:], two[8:]], axis=0).astype(BF16)
    for b in range(0, plane, 4):
        found = []
        for k in range(4):
            both = w_ref[b + k, pl.ds(16 * ring, 2 * padded), :].astype(F32)
            found.append(jnp.concatenate([both[:rows, :half], both[padded : padded + rows, :half]], axis=1))
        wd_ref[pl.ds(b * rows, 4 * rows), :] = jnp.concatenate(found, axis=0).astype(BF16)


def unpack_weights(weights, width, rows, before):
    plane, packed, ff = weights.shape
    return pl.pallas_call(
        unpack_kernel,
        in_specs=[IN_VMEM, ANYWHERE],
        out_specs=[IN_VMEM] * 3,
        out_shape=[
            jax.ShapeDtypeStruct((width, ff), BF16),
            jax.ShapeDtypeStruct((width, ff), BF16),
            jax.ShapeDtypeStruct((plane * rows, width), BF16),
        ],
        compiler_params=pltpu.CompilerParams(vmem_limit_bytes=20 * 2**20),
        cost_estimate=pl.CostEstimate(flops=0, bytes_accessed=8 * 10**6, transcendentals=0),
        name="unpack_weights",
    )(weights, before)


def feed_kernel(ids_ref, *refs):
    *near, far_ref, c_ref, wg_ref, wu_ref, wd_ref, h_ref, gg_ref, gu_ref, parts_ref, x_s = refs

    @pl.when(pl.program_id(0) == 0)
    def _():
        x_s[...] = jnp.concatenate([ref[...] for ref in near], axis=0)

    @pl.when(pl.program_id(0) == 1)
    def _():
        x_s[...] = far_ref[...]

    x = x_s[...]
    count = c_ref.shape[0] // ids_ref.shape[0]
    found = []
    for k in range(x.shape[0] // count):
        member = ids_ref[pl.program_id(0) * (x.shape[0] // count) + k]
        found.append(c_ref[pl.ds(pl.multiple_of(member * count, count), count), :])
    cotangent = jnp.concatenate(found, axis=0)
    gate_value = dot_nn(x, wg_ref[...])
    upward = dot_nn(x, wu_ref[...])
    grad_hidden = dot_nt(cotangent, wd_ref[...])
    sigmoid = 1.0 / (1.0 + jnp.exp(-gate_value))
    silu = gate_value * sigmoid
    h_ref[...] = (silu * upward).astype(BF16)
    grad_gate = (grad_hidden * upward * sigmoid * (1.0 + gate_value * (1.0 - sigmoid))).astype(BF16)
    grad_up = (grad_hidden * silu).astype(BF16)
    gg_ref[...] = grad_gate
    gu_ref[...] = grad_up
    parts_ref[...] = (dot_nt(grad_gate, wg_ref[...]) + dot_nt(grad_up, wu_ref[...])).astype(BF16)


def feed_back_kernel(ids_ref, *refs):
    *near, far_ref, h_ref, gg_ref, gu_ref, c_ref, wd_ref, _, raw_ref, down_ref = refs
    plane, packed, ff = raw_ref.shape
    members = ids_ref.shape[0]
    total, width = c_ref.shape
    padded = (packed - 16 * members) // 2
    rows = ff // plane
    per = far_ref.shape[1] // (8 * plane)
    turned = jnp.concatenate([transposed(ref[...]).astype(BF16) for ref in (*near, far_ref)], axis=1)
    part = total // pl.num_programs(0)
    count = total // members
    mine = h_ref[pl.ds(pl.multiple_of(pl.program_id(0) * part, part), part), :]
    mine = dot_nn(mine, wd_ref[...]).astype(BF16)
    for k in range(part // count):
        member = ids_ref[pl.program_id(0) * (part // count) + k]
        down_ref[pl.ds(pl.multiple_of(member * count, count), count), :] = mine[k * count : (k + 1) * count]
    gate = dot_nn(turned, gg_ref[...]).reshape(per, plane, 8, ff)
    up = dot_nn(turned, gu_ref[...]).reshape(per, plane, 8, ff)
    for k in range(per):
        at = pl.multiple_of((pl.program_id(0) * per + k) * 16, 16)
        raw_ref[:, pl.ds(at, 16), :] = jnp.concatenate([gate[k], up[k]], axis=1).astype(BF16)

    @pl.when(pl.program_id(0) == 0)
    def _():
        found = [c_ref[pl.ds(pl.multiple_of(ids_ref[k] * count, count), count), :] for k in range(members)]
        grad = dot_nn(transposed(h_ref[...]).astype(BF16), jnp.concatenate(found, axis=0))
        empty = jnp.zeros((padded - rows, ff), F32)
        beside = jnp.zeros((rows, ff - width // 2), F32)
        for b in range(plane):
            piece = grad[b * rows : (b + 1) * rows]
            stacked = []
            for k in range(2):
                part = piece[:, k * (width // 2) : (k + 1) * (width // 2)]
                stacked += [jnp.concatenate([part, beside], axis=1), empty]
            raw_ref[b, pl.ds(16 * members, 2 * padded), :] = jnp.concatenate(stacked, axis=0).astype(BF16)


def feed_forward(ids, near, far, cotangent, gate, up, down):
    total, width = cotangent.shape
    ff = gate.shape[1]
    rows = total // 2
    row = lambda i, ids: (i, 0)
    operands = (*near, far, cotangent, gate, up, down)
    return pl.pallas_call(
        feed_kernel,
        grid_spec=pltpu.PrefetchScalarGridSpec(
            num_scalar_prefetch=1,
            grid=(2,),
            in_specs=[pl.BlockSpec(part.shape, lambda i, ids: (0, 0)) for part in operands],
            out_specs=[pl.BlockSpec((rows, ff), row)] * 3 + [pl.BlockSpec((rows, width), row)],
            scratch_shapes=[pltpu.VMEM((rows, width), BF16)],
        ),
        out_shape=[jax.ShapeDtypeStruct((total, ff), BF16)] * 3 + [jax.ShapeDtypeStruct((total, width), BF16)],
        compiler_params=pltpu.CompilerParams(vmem_limit_bytes=40 * 2**20),
        cost_estimate=pl.CostEstimate(flops=8 * 10**9, bytes_accessed=15 * 10**6, transcendentals=10**6),
        name="feed_forward",
    )(ids, *operands)


def feed_back(ids, near, far, hidden, grad_gate, grad_up, cotangent, down, before, plane, packed):
    total, width = cotangent.shape
    ff = hidden.shape[1]
    steps = 2
    fixed = lambda i, ids: (0, 0)
    columns = lambda i, ids: (0, i)
    return pl.pallas_call(
        feed_back_kernel,
        grid_spec=pltpu.PrefetchScalarGridSpec(
            num_scalar_prefetch=1,
            grid=(steps,),
            in_specs=[pl.BlockSpec((part.shape[0], width // steps), columns) for part in (*near, far)]
            + [pl.BlockSpec(part.shape, fixed) for part in (hidden, grad_gate, grad_up, cotangent, down)]
            + [ANYWHERE],
            out_specs=[
                pl.BlockSpec((plane, packed, ff), lambda i, ids: (0, 0, 0)),
                pl.BlockSpec((total, width), fixed),
            ],
        ),
        out_shape=[
            jax.ShapeDtypeStruct((plane, packed, ff), BF16),
            jax.ShapeDtypeStruct((total, width), BF16),
        ],
        compiler_params=pltpu.CompilerParams(vmem_limit_bytes=52 * 2**20),
        cost_estimate=pl.CostEstimate(flops=5 * 10**9, bytes_accessed=15 * 10**6, transcendentals=0),
        name="feed_back",
    )(ids, *near, far, hidden, grad_gate, grad_up, cotangent, down, before)


def together(*values):
    return lax.optimization_barrier(values)


def ring_shift(values, axes, offset):
    return lax.ppermute(values, axes, [(i, (i - offset) % 4) for i in range(4)])


def other_core(values):
    return lax.ppermute(values, "c", [(0, 1), (1, 0)])


def near_ring(values):
    return [values] + [ring_shift(values, ("h", "l"), o) for o in OFFSETS[1:]]


def far_ring(near):
    return other_core(jnp.concatenate(near, axis=0))


def scatter_ring_first(parts):
    return (parts[:4].astype(F32) + other_core(parts[4:]).astype(F32)).astype(BF16)


def scatter_ring_second(mine):
    got = [ring_shift(mine[k], ("h", "l"), -OFFSETS[k]) for k in range(1, 4)]
    return [mine[0]] + got


def add_all(parts):
    total = parts[0].astype(F32)
    for part in parts[1:]:
        total = total + part.astype(F32)
    return total


def heads_to_tokens(values):
    parts = values.reshape(8, -1, values.shape[1])
    got = lax.all_to_all(parts, RING, split_axis=0, concat_axis=0, tiled=True)
    return got.transpose(1, 0, 2).reshape(parts.shape[1], -1)


def tokens_to_heads(values):
    parts = values.reshape(values.shape[0], 8, -1).transpose(1, 0, 2)
    got = lax.all_to_all(parts, RING, split_axis=0, concat_axis=0, tiled=True)
    return got.reshape(-1, parts.shape[2])


def gather_plane(values):
    half = values.shape[0] // 2
    first = [values[:half], values[half:]]
    lines = [[part] + [ring_shift(part, axis, o) for o in OFFSETS[1:]] for part, axis in zip(first, ("x", "z"))]
    lines = together(*[jnp.concatenate(line, axis=0) for line in lines])
    result = [[line] + [ring_shift(line, axis, o) for o in OFFSETS[1:]] for line, axis in zip(lines, ("z", "x"))]
    return result[0] + result[1]


def scatter_plane_first(pieces):
    parts = []
    for half, axis in ((pieces[:4], "z"), (pieces[4:], "x")):
        parts += [half[0]] + [ring_shift(half[k], axis, -OFFSETS[k]) for k in range(1, 4)]
    return parts


def scatter_plane_second(parts):
    lines = [add_all(parts[:4]).astype(BF16), add_all(parts[4:]).astype(BF16)]
    result = []
    for line, axis in zip(lines, ("x", "z")):
        part = line.reshape(4, -1, line.shape[1])
        result.append([part[0]] + [ring_shift(part[k], axis, -OFFSETS[k]) for k in range(1, 4)])
    return jnp.concatenate([add_all(parts) for parts in result], axis=0)


def rms(values):
    return lax.rsqrt(jnp.mean(values * values, axis=-1, keepdims=True) + EPS)


def rms_back(values, scale, upstream):
    inner = jnp.mean(values * upstream, axis=-1, keepdims=True)
    return scale * upstream - values * (scale * scale * scale) * inner


def to_all_plane(values):
    spread = jnp.broadcast_to(values[None], (16,) + values.shape)
    return lax.all_to_all(spread, PLANE, split_axis=0, concat_axis=0, tiled=True)


def sum_plane(parts):
    got = lax.all_to_all(parts.astype(BF16), PLANE, split_axis=0, concat_axis=0, tiled=True)
    return jnp.sum(got.astype(F32), axis=0)


def offset_of(slot):
    return jnp.where(slot == 1, -1, jnp.where(slot > 1, slot - 1, 0))


def places(span_order):
    me = lax.axis_index(AXES).astype(jnp.int32)
    number = jnp.arange(256, dtype=jnp.int32)
    device = me + jnp.zeros_like(number)
    half = number >> 7
    outer, inner = offset_of((number >> 5) & 3), offset_of((number >> 3) & 3)
    x = (((device >> 2) & 3) + jnp.where(half == 0, inner, outer)) & 3
    z = ((device & 3) + jnp.where(half == 0, outer, inner)) & 3
    member = half * 4 + ((number >> 1) & 3)
    span = 2 * (member * 16 + x * 4 + z) + (number & 1)
    streams = jnp.sum(jnp.where(span[:, None] == number[None, :], span_order[None, :], 0), axis=1)
    number = jnp.arange(8, dtype=jnp.int32)
    device = me + jnp.zeros_like(number)
    y = ((device >> 6) & 1) * 2 + ((device >> 4) & 1)
    y = (y + offset_of(number & 3)) & 3
    core = ((device >> 5) & 1) ^ (number >> 2)
    return streams, (y >> 1) * 4 + core * 2 + (y & 1)


def rotary_tables(blocks, starts):
    stream = (blocks[:, None] * SPAN + jnp.arange(SPAN, dtype=jnp.int32)[None, :]).reshape(-1, 1)
    begins = jnp.zeros_like(stream)
    for number in range(1, SEQS):
        begins = jnp.where(stream >= starts[number], starts[number], begins)
    inverse = jnp.power(THETA, -jnp.arange(0, HEAD_DIM, 2).astype(F32) / HEAD_DIM)
    angles = (stream - begins).astype(F32) * jnp.tile(inverse, 4)[None, :]
    return jnp.cos(angles), jnp.sin(angles)


def local(
    tokens, document_ids, span_order, attention_gain, head_gain, qkv_weight, out_weight,
    feed_gain, gate_weight, up_weight, down_weight, cotangent,
):
    rows, width = tokens.shape
    ring, plane = 8, 16
    down_rows = down_weight.shape[0]
    ff = down_rows * plane
    half = width // 2
    pad_rows, pad_columns = -down_rows % 8, ff - half
    near_tokens = near_ring(tokens)
    ring_cotangent = lax.all_gather(cotangent, RING, axis=0, tiled=True)

    starts = jnp.sum(
        (document_ids[None, :] < jnp.arange(SEQS, dtype=jnp.int32)[:, None]).astype(jnp.int32), axis=1
    )
    streams, ring_ids = places(span_order)
    own_blocks = jnp.concatenate([streams[:8], streams[128:136]])
    cosine, sine = rotary_tables(own_blocks, starts)
    items, tiles, groups = work_list(own_blocks, starts, document_ids.shape[0])
    tables = (streams, items, tiles, groups, starts)

    gain_a = attention_gain.astype(F32)[:, None]
    gain_f = feed_gain.astype(F32)[:, None]
    scaled_qkv = (gain_a * qkv_weight.astype(F32)).astype(BF16)
    qw, kw, vw = scaled_qkv[:, :1024], scaled_qkv[:, 1024:1536], scaled_qkv[:, 1536:]
    by_head = jnp.concatenate(
        [v.reshape(8, ring, -1).transpose(1, 0, 2) for v in (qw, kw, vw)], axis=2
    )
    gain_rows = jnp.broadcast_to(head_gain.reshape(1, 1, 1), (ring, 8, by_head.shape[2]))
    message = jnp.concatenate([by_head, gain_rows], axis=1)
    message = jnp.pad(message, ((0, 0), (0, 0), (0, ff - message.shape[2])))
    gate_up = jnp.stack([gate_weight, up_weight])
    scaled_gate_up = (gain_f * gate_up.astype(F32)).astype(BF16)
    feed_message = scaled_gate_up.reshape(2, 8, ring, ff).transpose(2, 0, 1, 3).reshape(ring, 16, ff)
    message = jnp.concatenate([message, feed_message], axis=1)
    message = lax.all_to_all(message, RING, split_axis=0, concat_axis=0, tiled=True)
    others = together(message, cosine, sine, *tables, *near_tokens)
    message, cosine, sine, tables, near_tokens = *others[:3], others[3:-4], others[-4:]
    far_tokens = far_ring(near_tokens)
    feed_message = message[:, 16:]
    message = message[:, :16, :256]
    head_gains = jnp.broadcast_to(message[:, 8, :1], (ring, 256))
    out_rows = out_weight.reshape(8, 4, 256).transpose(1, 0, 2).reshape(32, 256)
    message = jnp.concatenate([message[:, :8].reshape(ring * 8, -1), head_gains, out_rows], axis=0)
    gathered = to_all_plane(message)
    own_qkv = gathered[:, :64].reshape(plane, ring, 8, -1).transpose(1, 0, 2, 3).reshape(width, -1)
    gains = gathered[:, 64:72, 0].T.reshape(1, 2 * HEAD_DIM).astype(F32)
    gains = jnp.concatenate([gains[:, :HEAD_DIM], gains, jnp.ones((1, HEAD_DIM), F32)], axis=1)
    own_out = gathered[:, 72:].reshape(plane, 4, 8, 256).transpose(0, 2, 1, 3).reshape(8 * plane, width)
    all_out = lax.all_gather(own_out, RING, axis=0, tiled=True)

    ring_normed, projected, queries, key_values = project(
        ring_ids, near_tokens, far_tokens, own_qkv, cosine, sine, gains, ring_cotangent[:8, :128]
    )
    all_kv = gather_plane(key_values)
    down_halves = jnp.stack([down_weight[:, :half], down_weight[:, half:]])
    down_halves = jnp.pad(down_halves, ((0, 0), (0, pad_rows), (0, pad_columns)))
    message = jnp.concatenate([feed_message.reshape(ring * 16, ff), down_halves.reshape(-1, ff)], axis=0)
    feed_weights = lax.all_gather(message, PLANE, axis=0, tiled=True).reshape(plane, -1, ff)
    outputs, attended, logs = attention_forward(tables, queries, all_kv, all_out)
    head_outputs = heads_to_tokens(attended)
    residual = tokens.astype(F32) + dot_nn(head_outputs, all_out)
    feed_scale = rms(residual)
    feed_normed = (residual * feed_scale).astype(BF16)
    own_gate, own_up, own_down = unpack_weights(feed_weights, width, down_rows, feed_normed)
    near_feed = near_ring(feed_normed)
    far_feed = far_ring(near_feed)
    hidden, grad_gate, grad_up, feed_parts = feed_forward(
        ring_ids, near_feed, far_feed, ring_cotangent, own_gate, own_up, own_down
    )

    mine = scatter_ring_first(feed_parts.reshape(ring, rows, width))
    grad_feed = scatter_ring_second(mine)
    raw, down_parts = feed_back(
        ring_ids, near_feed, far_feed, hidden, grad_gate, grad_up, ring_cotangent, own_down, mine,
        plane, message.shape[0],
    )
    *grad_feed, raw = together(*grad_feed, raw)
    grad_residual = cotangent.astype(F32) + rms_back(residual, feed_scale, add_all(grad_feed))
    grad_attended = grad_residual.astype(BF16)
    raw = lax.psum_scatter(raw.reshape(-1, ff), PLANE, scatter_dimension=0, tiled=True)
    grad_heads = tokens_to_heads(dot_nt(grad_attended, all_out).astype(BF16))

    near_attended = near_ring(grad_attended)

    grad_queries, *grad_kv_parts = attention_backward(
        tables, queries, grad_heads, outputs, logs, all_kv
    )
    others = together(*grad_kv_parts, *near_attended, down_parts)
    grad_kv_parts, near_attended, down_parts = others[:PIECES], others[PIECES:-1], others[-1]
    output_sum = lax.psum_scatter(down_parts, RING, scatter_dimension=0, tiled=True)
    others = together(*scatter_plane_first(grad_kv_parts), *near_attended)
    parts, near_attended = others[:PIECES], others[PIECES:]
    grad_kv = scatter_plane_second(parts)
    grad_out = out_back(ring_ids, attended, near_attended, far_ring(near_attended))
    grad_kv, raw = together(grad_kv, raw)
    grad_projected, norm_parts, grad_gains = project_back(
        ring_ids, grad_queries, grad_kv, projected, cosine, sine, gains, own_qkv
    )
    mine = scatter_ring_first(norm_parts.reshape(ring, rows, width))

    back = dot_tn(ring_normed, grad_projected).astype(BF16)
    back = back.reshape(ring, plane, 8, -1).transpose(1, 0, 2, 3).reshape(plane, ring * 8, -1)
    grad_gains = jnp.sum(grad_gains, axis=0)
    grad_gains = jnp.concatenate([grad_gains[:64] + grad_gains[64:128], grad_gains[128:192]])
    gain_part = grad_gains.reshape(ring, plane).T.reshape(plane, ring, 1).astype(BF16)
    gain_part = jnp.broadcast_to(gain_part, (plane, ring, 256))
    grad_out = grad_out.reshape(plane, 8, 4, 256).transpose(0, 2, 1, 3).reshape(plane, 32, 256)
    back = jnp.concatenate([back, gain_part, grad_out], axis=1)
    mine, back = together(mine, back)
    grad_norm = scatter_ring_second(mine)
    back = sum_plane(back)
    *grad_norm, back = together(*grad_norm, back)
    own_tokens = tokens.astype(F32)
    grad_tokens = grad_residual + rms_back(own_tokens, rms(own_tokens), add_all(grad_norm))
    grad_out = back[72:].reshape(4, 8, 256).transpose(1, 0, 2).reshape(8, width)
    gain_part = jnp.broadcast_to(back[64:72, None], (ring, 8, 256))
    back = jnp.concatenate([back[:64].reshape(ring, 8, 256), gain_part], axis=1).astype(BF16)
    back = jnp.pad(back, ((0, 0), (0, 0), (0, ff - back.shape[2])))
    back = jnp.concatenate([back, raw[: ring * 16].reshape(ring, 16, ff)], axis=1)
    block_output = (residual + output_sum.astype(F32)).astype(BF16)
    back = lax.all_to_all(back, RING, split_axis=0, concat_axis=0, tiled=True).astype(F32)
    back, raw_back = back[:, :16, :256], back[:, 16:]
    grad_head_gain = jnp.sum(back[:, 8, 0]).reshape(1)
    back = back[:, :8].transpose(1, 0, 2)
    back = jnp.concatenate(
        [back[:, :, lo:hi].reshape(8, -1) for lo, hi in ((0, 128), (128, 192), (192, 256))], axis=1
    )
    grad_qkv_weight = gain_a * back
    grad_attention_gain = jnp.sum(back * qkv_weight.astype(F32), axis=1)

    raw_down = raw[ring * 16 :].reshape(2, -1, ff)[:, :down_rows, :half]
    grad_down = jnp.concatenate([raw_down[0], raw_down[1]], axis=1).astype(F32)
    raw = raw_back.reshape(ring, 2, 8, ff).transpose(1, 2, 0, 3).reshape(2, 8, ring * ff)
    grad_gate_weight, grad_up_weight = gain_f * raw[0], gain_f * raw[1]
    grad_feed_gain = jnp.sum(raw * gate_up.astype(F32), axis=(0, 2))
    return (
        block_output, grad_tokens, grad_attention_gain, grad_head_gain, grad_qkv_weight, grad_out,
        grad_feed_gain, grad_gate_weight, grad_up_weight, grad_down,
    )


def solution(mesh):
    fine = Mesh(mesh.devices.reshape(2, 2, 2, 4, 4), AXES)
    one, two, whole = P(AXES), P(AXES, None), P()
    in_specs = (two, whole, whole, one, one, two, two, one, two, two, two, two)
    out_specs = (two, two, one, one, two, two, one, two, two, two)
    return jax.shard_map(local, mesh=fine, in_specs=in_specs, out_specs=out_specs, check_vma=False)
```
